32 devices in a mesh: row: 4 (over z), col: 8 (over y, x, core).
Axes of the slice: x: 2, y: 2, z: 4, core: 2. Of those that a mesh axis runs over, the one named last changes fastest.
Arguments:
- x_vec: float32 [4, 524288], P(None, ('col', 'row'))
- hx_vec: float32 [4, 524288], P(None, ('col', 'row'))
- p_vec: float32 [4, 524288], P(None, ('col', 'row'))
- hp_vec: float32 [4, 524288], P(None, ('col', 'row'))
- theta: float32 [4], replicated, may hold values from 0.5 to 2
- precond: float32 [524288], P(('col', 'row')), may hold values from 1 to 4
- tile_vals: bfloat16 [4, 8, 1024, 4096], P('row', 'col'), may hold values from -0.25 to 0.25
- tile_rows: int32 [4, 8, 1024], P('row', 'col'), may hold values from 0 to 1023
- tile_cols: int32 [4, 8, 1024], P('row', 'col'), may hold values from 0 to 1023
- tile_count: int32 [4, 8], P('row', 'col'), may hold values from 128 to 1024, as said below
Outputs:
- hw_vec: float32 [4, 524288], P(None, ('col', 'row'))
- gram_a: float32 [12, 12], replicated
- gram_b: float32 [12, 12], replicated
The draws below stay inside these ranges and needn't reach their ends.
Inputs may be any that keep to these rules, and one draw needn't show every extreme that they name: `tile_count`: some tile uses all 1024 slots and some tile uses 1024 // 8.
All inputs are finite; a program needn't handle non-finite values.
Results may differ from the reference program's by a relative error of at most 0.0029.
Values may be sent and summed in bfloat16 or wider, within the bound.
A program may use at most 192 MiB of HBM per device.

```python
import math
import jax
import jax.numpy as jnp
from jax import lax

VECS = 4
BLOCK = 64
PIECE = 16384
NZ = 1024
NBLK = 1024
NDIM = 524288
N_ROW = 4
N_COL = 8


def shared_normal(key):
    return jax.random.normal(key, (VECS, NDIM), jnp.float32)


def paired_normal(key):
    pair_key = jax.random.fold_in(key, 101)
    return jnp.clip(jax.random.normal(pair_key, (VECS, NDIM), jnp.float32), -6.0, 6.0)


def rising_envelope():
    return jnp.exp(jnp.log(3.0) * jnp.arange(NDIM, dtype=jnp.float32) / NDIM) / 1.7


def draw_x_vec(key, part):
    shaped = shared_normal(key)
    return rising_envelope()[None, :] * shaped


def draw_hx_vec(key, part):
    shaped = shared_normal(key)
    key = jax.random.fold_in(key, 5)
    noise = jax.random.normal(key, (VECS, NDIM), jnp.float32)
    return rising_envelope()[None, :] * 1.5 * shaped + 0.8 * noise


def draw_p_vec(key, part):
    shaped = paired_normal(key)
    return shaped


def draw_hp_vec(key, part):
    shaped = paired_normal(key)
    key = jax.random.fold_in(key, 13)
    factor_key, noise_key = jax.random.split(key)
    factors = jax.random.uniform(factor_key, (VECS,), jnp.float32, 0.6, 1.6)
    noise = jax.random.normal(noise_key, (VECS, NDIM), jnp.float32)
    return factors[:, None] * shaped + 0.8 * noise


def draw_tile_count(key, part):
    key = jax.random.fold_in(key, 11)
    first_key, second_key = jax.random.split(key)
    total = N_ROW * N_COL
    counts = jax.random.randint(first_key, (total,), NZ // 8, NZ + 1)
    fullest = jax.random.randint(second_key, (), 0, total)
    places = jnp.arange(total, dtype=jnp.int32)
    counts = jnp.where(places == fullest, NZ, counts)
    counts = jnp.where(places == (fullest + 1) % total, NZ // 8, counts)
    return counts.reshape(N_ROW, N_COL).astype(jnp.int32)


def touch_ends(entries, stream_key, smallest, largest):
    shape = entries.shape
    place = [jax.random.randint(jax.random.fold_in(stream_key, axis), (), 0, shape[axis]) for axis in range(len(shape))]
    entries = entries.at[tuple(place)].set(smallest)
    longest = shape.index(max(shape))
    place[longest] = (place[longest] + 1) % shape[longest]
    return entries.at[tuple(place)].set(largest)


def block_scale(stream_key, dims, pieces, smallest, top_value):
    gain, own = 1.0, jax.random.fold_in(stream_key, 6)
    for axis_at, shards_of in pieces:
        draws = jnp.exp(jax.random.uniform(jax.random.fold_in(own, axis_at), (shards_of,), jnp.float32, smallest / len(pieces), top_value / len(pieces)))
        gain = gain * jnp.repeat(draws, dims[axis_at] // shards_of).reshape([-1 if axis == axis_at else 1 for axis in range(len(dims))])
    return gain


def centred(own_key, shape, scale, bound, pieces=(), kind=jnp.bfloat16):
    array = scale * jax.random.normal(own_key, shape, jnp.float32)
    if pieces:
        array = array * block_scale(own_key, shape, pieces, -0.22, 0.18)
    return jnp.clip(array, -bound, bound).astype(kind)


def setup_inputs(seed: int = 0) -> dict:
    streams_of = jax.random.split(jax.random.key(seed), 11)
    return {
        "x_vec": draw_x_vec(jax.random.fold_in(streams_of[10], 71), 0),
        "hx_vec": draw_hx_vec(jax.random.fold_in(streams_of[10], 71), 0),
        "p_vec": draw_p_vec(jax.random.fold_in(streams_of[10], 71), 0),
        "hp_vec": draw_hp_vec(jax.random.fold_in(streams_of[10], 71), 0),
        "theta": jnp.clip(jax.random.uniform(streams_of[4], (VECS,), jnp.float32, 0.5, 2.0), 0.5, 2.0),
        "precond": jnp.clip(jnp.exp(math.log(4.0) - 1.3862944 * jax.random.uniform(streams_of[5], (NDIM,), jnp.float32) ** block_scale(streams_of[5], (NDIM,), ((0, 32),), -0.2, 0.2)), 1.0, 4.0),
        "tile_vals": centred(streams_of[6], (N_ROW, N_COL, NZ, BLOCK * BLOCK), (2 * NZ * BLOCK * BLOCK // PIECE) ** -0.5, 0.25, ((0, 4), (1, 8))),
        "tile_rows": touch_ends(jax.random.randint(streams_of[7], (N_ROW, N_COL, NZ), 0, NBLK), jax.random.fold_in(streams_of[7], 1), 0, NBLK - 1).astype(jnp.int32),
        "tile_cols": touch_ends(jax.random.randint(streams_of[8], (N_ROW, N_COL, NZ), 0, NBLK), jax.random.fold_in(streams_of[8], 1), 0, NBLK - 1).astype(jnp.int32),
        "tile_count": draw_tile_count(jax.random.fold_in(streams_of[10], 71), 0),
    }


def segment_blocks(part, index, block_total):
    summed = jax.ops.segment_sum(part, index, num_segments=block_total)
    return jnp.transpose(summed, (1, 0, 2)).reshape(part.shape[1], -1)


def tile_terms(flat_values, row_index, col_index, live_mask, col_vec, row_vec):
    vec_count = col_vec.shape[0]
    values = flat_values.reshape(flat_values.shape[0], BLOCK, BLOCK)
    blocks_col = col_vec.reshape(vec_count, -1, BLOCK)
    blocks_row = row_vec.reshape(vec_count, -1, BLOCK)
    block_total = blocks_col.shape[1]
    picked_col = blocks_col[:, col_index, :].astype(jnp.float32)
    picked_row = blocks_row[:, row_index, :].astype(jnp.float32)
    wide = values.astype(jnp.float32)
    forward_part = jnp.einsum('zij,kzj->zki', wide, picked_col, precision=lax.Precision.HIGHEST) * live_mask[:, None, None]
    transpose_part = jnp.einsum('zij,kzi->zkj', wide, picked_row, precision=lax.Precision.HIGHEST) * live_mask[:, None, None]
    return segment_blocks(forward_part, row_index, block_total), segment_blocks(transpose_part, col_index, block_total)


def reference(x_vec, hx_vec, p_vec, hp_vec, theta, precond, tile_vals, tile_rows, tile_cols, tile_count):
    residue = (hx_vec - x_vec * theta[:, None]) / precond[None, :]
    w_send = residue.astype(jnp.bfloat16)
    seg_len = PIECE * N_ROW
    segments = w_send.reshape(VECS, N_COL, seg_len)

    def visit(tile_pos, accum):
        row_pos = tile_pos // N_COL
        col_pos = tile_pos % N_COL
        target = (col_pos + row_pos) % N_COL
        live_mask = (jnp.arange(NZ, dtype=jnp.int32) < tile_count[row_pos, col_pos]).astype(jnp.float32)
        forward_seg, transpose_seg = tile_terms(tile_vals[row_pos, col_pos], tile_rows[row_pos, col_pos], tile_cols[row_pos, col_pos], live_mask, segments[:, col_pos], segments[:, target])
        accum = accum.at[:, target].add(forward_seg)
        return accum.at[:, col_pos].add(transpose_seg)

    accum = lax.fori_loop(0, N_ROW * N_COL, visit, jnp.zeros((VECS, N_COL, seg_len), jnp.float32))
    hw_vec = accum.reshape(VECS, NDIM)
    vectors = jnp.concatenate([x_vec, residue, p_vec], 0)
    images = jnp.concatenate([hx_vec, hw_vec, hp_vec], 0)
    gram_a = jnp.dot(vectors, images.T, precision=lax.Precision.HIGHEST, preferred_element_type=jnp.float32) / NDIM
    gram_b = jnp.dot(vectors, vectors.T, precision=lax.Precision.HIGHEST, preferred_element_type=jnp.float32) / NDIM
    return hw_vec, gram_a, gram_b
```

```python
import functools
import jax
import jax.numpy as jnp
from jax import lax
from jax.experimental import pallas as pl
from jax.experimental.pallas import tpu as pltpu
from jax.sharding import PartitionSpec as P

BLOCK = 64
GROUPS = 4
MESH = pl.DeviceIdType.MESH
F32 = jnp.float32
BF16 = jnp.bfloat16
VMEM_BYTES = 58 * 1024 * 1024


def row_iota():
    return lax.broadcasted_iota(jnp.int32, (8, 128), 0)


def lane_iota():
    return lax.broadcasted_iota(jnp.int32, (8, 128), 1)


def spread_matrix():
    a = lax.broadcasted_iota(jnp.int32, (128, 128), 0)
    b = lax.broadcasted_iota(jnp.int32, (128, 128), 1)
    return jnp.where((a % 64) == 2 * (b % 32) + a // 64, 1.0, 0.0).astype(BF16)


def gather_kernel(w_ref, own_ref, far_ref, up_send, up_recv, down_send, down_recv, far_send, far_recv):
    n = own_ref.shape[0]
    cols = lax.axis_size("col")
    r, c = lax.axis_index("row"), lax.axis_index("col")
    source = lax.rem(c + r, cols)
    target = lax.rem(c - r + cols, cols)
    barrier = pltpu.get_barrier_semaphore()

    def greet(row, col):
        pl.semaphore_signal(barrier, inc=1, device_id=(row, col), device_id_type=MESH)

    pl.when(r > 0)(lambda: greet(r - 1, c))
    pl.when(r < n - 1)(lambda: greet(r + 1, c))
    pl.when(r > 0)(lambda: greet(r, source))
    own_ref[r] = w_ref[...]
    pl.semaphore_wait(barrier, jnp.where(r > 0, jnp.where(r < n - 1, 3, 2), 1))

    def up_copy(piece, d):
        return pltpu.make_async_remote_copy(
            src_ref=own_ref.at[piece], dst_ref=own_ref.at[piece],
            send_sem=up_send.at[d], recv_sem=up_recv.at[d],
            device_id=(r + 1, c), device_id_type=MESH)

    def down_copy(piece, d):
        return pltpu.make_async_remote_copy(
            src_ref=own_ref.at[piece], dst_ref=own_ref.at[piece],
            send_sem=down_send.at[d], recv_sem=down_recv.at[d],
            device_id=(r - 1, c), device_id_type=MESH)

    def far_copy(piece, slot):
        return pltpu.make_async_remote_copy(
            src_ref=own_ref.at[piece], dst_ref=far_ref.at[piece],
            send_sem=far_send.at[slot], recv_sem=far_recv.at[slot],
            device_id=(r, target), device_id_type=MESH)

    pl.when(r < n - 1)(lambda: up_copy(r, 0).start())
    pl.when(r > 0)(lambda: down_copy(r, 0).start())
    pl.when(r > 0)(lambda: far_copy(r, 0).start())
    for d in range(1, n):
        @pl.when(r >= d)
        def _():
            up_copy(r - d, d - 1).wait_recv()
            pl.when(r < n - 1)(lambda: up_copy(r - d, d).start())
            far_copy(r - d, 2 * d - 1).start()

        @pl.when(r + d < n)
        def _():
            down_copy(r + d, d - 1).wait_recv()

            @pl.when(r > 0)
            def _():
                down_copy(r + d, d).start()
                far_copy(r + d, 2 * d).start()

    @pl.when(r == 0)
    def _():
        far_ref[...] = own_ref[...]

    for d in range(n):
        if d:
            @pl.when(r >= d)
            def _():
                far_copy(r - d, 2 * d - 1).wait()

            @pl.when((r + d < n) & (r > 0))
            def _():
                far_copy(r + d, 2 * d).wait()

            pl.when((r >= d) & (r < n - 1))(lambda: up_copy(r - d, d).wait_send())
            pl.when((r + d < n) & (r > 0))(lambda: down_copy(r + d, d).wait_send())
        else:
            pl.when(r > 0)(lambda: far_copy(r, 0).wait())
            pl.when(r < n - 1)(lambda: up_copy(r, 0).wait_send())
            pl.when(r > 0)(lambda: down_copy(r, 0).wait_send())


def gather_pieces(piece, n):
    shape = jax.ShapeDtypeStruct((n,) + piece.shape, piece.dtype)
    vmem = pl.BlockSpec(memory_space=pltpu.VMEM)
    dma = pltpu.SemaphoreType.DMA
    return pl.pallas_call(
        gather_kernel,
        out_shape=(shape, shape),
        in_specs=[vmem],
        out_specs=(vmem, vmem),
        scratch_shapes=[dma((n,)), dma((n,)), dma((n,)), dma((n,)), dma((2 * n,)), dma((2 * n,))],
        compiler_params=pltpu.CompilerParams(
            collective_id=0, has_side_effects=True, vmem_limit_bytes=VMEM_BYTES),
    )(piece)


def product_kernel(chunk, rows_ref, cols_ref, count_ref, vals_ref, own_ref, far_ref, fwd_ref, tr_ref,
                   x_col, x_row, acc_f, acc_t):
    step, steps = pl.program_id(0), pl.num_programs(0)
    n, _, width = own_ref.shape
    tiles = width // 128
    per_group = 2 * tiles
    nblk = n * GROUPS * per_group
    low = row_iota() < 4
    left = lane_iota() < 64
    keep = low == left
    quarter = lane_iota() // 32

    def block_at(q, g, t, parity):
        return q * (GROUPS * per_group) + g * per_group + 2 * t + parity

    def expand(src_ref, dst_ref):
        def tile(i, _):
            q, t = i // tiles, i % tiles
            s = src_ref[q, :, pl.ds(pl.multiple_of(t * 128, 128), 128)].astype(F32)
            for h in range(2):
                v = s[8 * h:8 * h + 8]
                vl = pltpu.roll(v, 64, 1)
                vs = pltpu.roll(v, 4, 0)
                vls = pltpu.roll(vl, 4, 0)
                dst_ref[block_at(q, 2 * h, t, 0)] = jnp.where(keep, jnp.where(low, v, vls), 0.0)
                dst_ref[block_at(q, 2 * h, t, 1)] = jnp.where(keep, jnp.where(low, vl, vs), 0.0)
                dst_ref[block_at(q, 2 * h + 1, t, 0)] = jnp.where(keep, jnp.where(low, vs, vl), 0.0)
                dst_ref[block_at(q, 2 * h + 1, t, 1)] = jnp.where(keep, jnp.where(low, vls, v), 0.0)
            return 0
        lax.fori_loop(0, n * tiles, tile, 0, unroll=4)

    @pl.when(step == 0)
    def _():
        expand(own_ref, x_col)
        expand(far_ref, x_row)
        spread = spread_matrix()

        def part(i, _):
            at = pl.ds(i * 32, 32)
            x = x_row[at].reshape(256, 128).astype(BF16)
            x_row[at] = jnp.dot(x, spread, preferred_element_type=F32).reshape(32, 8, 128)
            zero = jnp.zeros((32, 8, 128), F32)
            acc_f[at] = zero
            acc_t[at] = zero
            return 0
        lax.fori_loop(0, nblk // 32, part, 0)

    count = count_ref[0]
    first = step * chunk
    live = jnp.clip(count - first, 0, chunk)

    def octet(i, _):
        for half in range(2):
            at = i * 8 + half * 4
            w = vals_ref[pl.ds(pl.multiple_of(at * 32, 128), 128), :]
            rows, cols, lf, lt = [], [], [], []
            for z in range(4):
                slot = first + at + z
                r, c = rows_ref[slot], cols_ref[slot]
                lf.append(x_col[c])
                lt.append(jnp.where(quarter == z, x_row[r], 0.0))
                used = slot < count
                rows.append(jnp.where(used, r, nblk))
                cols.append(jnp.where(used, c, nblk))
            of = lax.dot_general(jnp.concatenate(lf, 0).astype(BF16), w, (((1,), (1,)), ((), ())),
                                 preferred_element_type=F32)
            ot = jnp.dot(jnp.concatenate(lt, 0).astype(BF16), w, preferred_element_type=F32)
            for z in range(4):
                acc_f[rows[z]] += jnp.where(quarter == z, of[8 * z:8 * z + 8], 0.0)
                acc_t[cols[z]] += ot[8 * z:8 * z + 8]
        return 0
    lax.fori_loop(0, (live + 7) // 8, octet, 0)

    @pl.when(step == steps - 1)
    def _():
        spread = spread_matrix()

        def part(i, _):
            at = pl.ds(i * 32, 32)
            x = acc_f[at].reshape(256, 128)
            hi = x.astype(BF16)
            lo = (x - hi.astype(F32)).astype(BF16)
            back = (((1,), (1,)), ((), ()))
            y = lax.dot_general(hi, spread, back, preferred_element_type=F32)
            y += lax.dot_general(lo, spread, back, preferred_element_type=F32)
            acc_f[at] = y.reshape(32, 8, 128)
            return 0
        lax.fori_loop(0, nblk // 32, part, 0)

        def fold(src_ref, dst_ref):
            def folded(q, g, t, parity):
                x = jnp.where(keep, src_ref[block_at(q, g, t, parity)], 0.0)
                return x + pltpu.roll(pltpu.roll(x, 64, 1), 4, 0)

            def tile(i, _):
                q, t = i // tiles, i % tiles
                out = []
                for h in range(2):
                    e0, o0 = folded(q, 2 * h, t, 0), folded(q, 2 * h, t, 1)
                    e1, o1 = folded(q, 2 * h + 1, t, 0), folded(q, 2 * h + 1, t, 1)
                    top = jnp.where(left, e0, pltpu.roll(o0, 4, 0))
                    bottom = jnp.where(left, pltpu.roll(e1, 4, 0), o1)
                    out.append(jnp.where(low, top, bottom))
                at = pl.ds(pl.multiple_of(t * 128, 128), 128)
                dst_ref[q, :, at] = jnp.concatenate(out, 0).astype(dst_ref.dtype)
                return 0
            lax.fori_loop(0, n * tiles, tile, 0, unroll=4)

        fold(acc_f, fwd_ref)
        fold(acc_t, tr_ref)


def block_products(vals, rows, cols, count, own, far):
    slots = rows.shape[0]
    chunk = 64
    n, depth, width = own.shape
    nblk = n * GROUPS * (width // 64)
    whole = pl.BlockSpec((n, depth, width), lambda i, *_: (0, 0, 0))
    return pl.pallas_call(
        functools.partial(product_kernel, chunk),
        out_shape=(jax.ShapeDtypeStruct(own.shape, BF16), jax.ShapeDtypeStruct(own.shape, F32)),
        grid_spec=pltpu.PrefetchScalarGridSpec(
            num_scalar_prefetch=3,
            grid=(slots // chunk,),
            in_specs=[pl.BlockSpec((chunk * 32, 128), lambda i, *_: (i, 0)), whole, whole],
            out_specs=(whole, whole),
            scratch_shapes=[
                pltpu.VMEM((nblk, 8, 128), F32),
                pltpu.VMEM((nblk, 8, 128), F32),
                pltpu.VMEM((nblk + 1, 8, 128), F32),
                pltpu.VMEM((nblk + 1, 8, 128), F32),
            ],
        ),
        compiler_params=pltpu.CompilerParams(vmem_limit_bytes=VMEM_BYTES),
    )(rows, cols, count, vals, own, far)


def reduce_kernel(fwd_ref, tr_ref, out_ref, far, stage, landed, far_send, far_recv, send, recv):
    n = fwd_ref.shape[0]
    cols = lax.axis_size("col")
    r, c = lax.axis_index("row"), lax.axis_index("col")
    target = lax.rem(c + r, cols)
    source = lax.rem(c - r + cols, cols)
    barrier = pltpu.get_barrier_semaphore()
    for d in range(1, n):
        pl.semaphore_signal(barrier, inc=1, device_id=(lax.rem(r + d, n), c), device_id_type=MESH)

    @pl.when(r > 0)
    def _():
        pl.semaphore_signal(barrier, inc=1, device_id=(r, source), device_id_type=MESH)
    pl.semaphore_wait(barrier, jnp.where(r > 0, n, n - 1))

    def far_copy(d):
        q = lax.rem(r + d, n)
        return pltpu.make_async_remote_copy(
            src_ref=fwd_ref.at[q], dst_ref=far.at[q],
            send_sem=far_send.at[d], recv_sem=far_recv.at[d],
            device_id=(r, target), device_id_type=MESH)

    def row_copy(d):
        return pltpu.make_async_remote_copy(
            src_ref=stage.at[d - 1], dst_ref=landed.at[d - 1],
            send_sem=send.at[d - 1], recv_sem=recv.at[d - 1],
            device_id=(lax.rem(r + d, n), c), device_id_type=MESH)

    order = list(range(1, n)) + [0]

    @pl.when(r > 0)
    def _():
        for d in order:
            far_copy(d).start()

    @pl.when(r == 0)
    def _():
        far[...] = fwd_ref[...]

    for d in order:
        pl.when(r > 0)(lambda: far_copy(d).wait_recv())
        q = lax.rem(r + d, n)
        total = tr_ref[q] + far[q].astype(F32)
        if d:
            stage[d - 1] = total.astype(BF16)
            row_copy(d).start()
    for d in range(1, n):
        row_copy(d).wait_recv()
        total += landed[d - 1].astype(F32)
    width = total.shape[1]
    for g in range(GROUPS):
        out_ref[:, g * width:(g + 1) * width] = total[4 * g:4 * g + 4]
    for d in range(1, n):
        row_copy(d).wait_send()

    @pl.when(r > 0)
    def _():
        for d in order:
            far_copy(d).wait_send()


def reduce_pieces(fwd, tr):
    n, depth, width = fwd.shape
    vmem = pl.BlockSpec(memory_space=pltpu.VMEM)
    dma = pltpu.SemaphoreType.DMA
    return pl.pallas_call(
        reduce_kernel,
        out_shape=jax.ShapeDtypeStruct((depth // GROUPS, GROUPS * width), F32),
        in_specs=[vmem, vmem],
        out_specs=vmem,
        scratch_shapes=[
            pltpu.VMEM((n, depth, width), BF16),
            pltpu.VMEM((n - 1, depth, width), BF16),
            pltpu.VMEM((n - 1, depth, width), BF16),
            dma((n,)), dma((n,)), dma((n - 1,)), dma((n - 1,)),
        ],
        compiler_params=pltpu.CompilerParams(
            collective_id=1, has_side_effects=True, vmem_limit_bytes=VMEM_BYTES),
    )(fwd, tr)


def total_kernel(part_ref, out_ref, slots, send, recv):
    rows, cols = lax.axis_size("row"), lax.axis_size("col")
    count = rows * cols
    r, c = lax.axis_index("row"), lax.axis_index("col")
    me = r * cols + c
    barrier = pltpu.get_barrier_semaphore()

    def peer(d):
        other = lax.rem(me + d, count)
        return (other // cols, lax.rem(other, cols))

    def greet(d, _):
        pl.semaphore_signal(barrier, inc=1, device_id=peer(d), device_id_type=MESH)
        return 0
    lax.fori_loop(1, count, greet, 0)
    slots[me] = part_ref[...]
    pl.semaphore_wait(barrier, count - 1)

    def copy(d):
        return pltpu.make_async_remote_copy(
            src_ref=part_ref, dst_ref=slots.at[me],
            send_sem=send.at[d], recv_sem=recv.at[d],
            device_id=peer(d), device_id_type=MESH)

    def start(d, _):
        copy(d).start()
        return 0

    def finish(d, _):
        copy(d).wait()
        return 0
    lax.fori_loop(1, count, start, 0)
    lax.fori_loop(1, count, finish, 0)
    out_ref[...] = jnp.sum(slots[...], axis=0)


def total_over_devices(part, count):
    vmem = pl.BlockSpec(memory_space=pltpu.VMEM)
    dma = pltpu.SemaphoreType.DMA
    return pl.pallas_call(
        total_kernel,
        out_shape=jax.ShapeDtypeStruct(part.shape, F32),
        in_specs=[vmem],
        out_specs=vmem,
        scratch_shapes=[pltpu.VMEM((count,) + part.shape, F32), dma((count,)), dma((count,))],
        compiler_params=pltpu.CompilerParams(
            collective_id=2, has_side_effects=True, vmem_limit_bytes=VMEM_BYTES),
    )(part)


def body(x_vec, hx_vec, p_vec, hp_vec, theta, precond, tile_vals, tile_rows, tile_cols, tile_count):
    vec_count, piece_len = x_vec.shape
    row_count = lax.axis_size("row")
    col_count = lax.axis_size("col")
    ndim_total = piece_len * row_count * col_count
    residue = (hx_vec - x_vec * theta[:, None]) / precond[None, :]
    width = piece_len // GROUPS
    w_send = residue.astype(BF16).reshape(vec_count, GROUPS, width)
    w_send = jnp.transpose(w_send, (1, 0, 2)).reshape(GROUPS * vec_count, width)
    slot_total = tile_vals.shape[2]
    vals = tile_vals.reshape(slot_total * BLOCK * BLOCK // 128, 128)
    own, far = gather_pieces(w_send, row_count)
    fwd, tr = block_products(vals, tile_rows[0, 0], tile_cols[0, 0], tile_count[0], own, far)
    hw_vec = reduce_pieces(fwd, tr)
    vectors = jnp.concatenate([x_vec, residue, p_vec], 0)
    images = jnp.concatenate([hx_vec, hw_vec, hp_vec], 0)
    dims = (((1,), (1,)), ((), ()))
    local_a = lax.dot_general(vectors, images, dims, precision=lax.Precision.HIGHEST,
                              preferred_element_type=F32)
    local_b = lax.dot_general(vectors, vectors, dims, precision=lax.Precision.HIGHEST,
                              preferred_element_type=F32)
    rows = vectors.shape[0]
    part = jnp.zeros((32, 128), F32).at[:rows, :rows].set(local_a).at[16:16 + rows, :rows].set(local_b)
    total = total_over_devices(part, row_count * col_count) / ndim_total
    return (hw_vec, total[:rows, :rows], total[16:16 + rows, :rows])


def solution(mesh):
    placed = (
        P(None, ("col", "row")),
        P(None, ("col", "row")),
        P(None, ("col", "row")),
        P(None, ("col", "row")),
        P(),
        P(("col", "row")),
        P("row", "col", None, None),
        P("row", "col", None),
        P("row", "col", None),
        P("row", "col"),
    )
    return jax.shard_map(
        body,
        mesh=mesh,
        in_specs=placed,
        out_specs=(P(None, ("col", "row")), P(), P()),
        check_vma=False,
    )
```

```python
import functools
import jax
import jax.numpy as jnp
from jax import lax
from jax.experimental import pallas as pl
from jax.experimental.pallas import tpu as pltpu
from jax.sharding import PartitionSpec as P

BLOCK = 64
GROUPS = 4
MESH = pl.DeviceIdType.MESH
F32 = jnp.float32
BF16 = jnp.bfloat16
VMEM_BYTES = 58 * 1024 * 1024


def row_iota():
    return lax.broadcasted_iota(jnp.int32, (8, 128), 0)


def lane_iota():
    return lax.broadcasted_iota(jnp.int32, (8, 128), 1)


def spread_matrix():
    a = lax.broadcasted_iota(jnp.int32, (128, 128), 0)
    b = lax.broadcasted_iota(jnp.int32, (128, 128), 1)
    return jnp.where((a % 64) == 2 * (b % 32) + a // 64, 1.0, 0.0).astype(BF16)


def gather_kernel(w_ref, own_ref, far_ref, up_send, up_recv, down_send, down_recv, far_send, far_recv):
    n = own_ref.shape[0]
    cols = lax.axis_size("col")
    r, c = lax.axis_index("row"), lax.axis_index("col")
    source = lax.rem(c + r, cols)
    target = lax.rem(c - r + cols, cols)
    barrier = pltpu.get_barrier_semaphore()

    def greet(row, col):
        pl.semaphore_signal(barrier, inc=1, device_id=(row, col), device_id_type=MESH)

    pl.when(r > 0)(lambda: greet(r - 1, c))
    pl.when(r < n - 1)(lambda: greet(r + 1, c))
    pl.when(r > 0)(lambda: greet(r, source))
    own_ref[r] = w_ref[...]
    pl.semaphore_wait(barrier, jnp.where(r > 0, jnp.where(r < n - 1, 3, 2), 1))

    def up_copy(piece, d):
        return pltpu.make_async_remote_copy(
            src_ref=own_ref.at[piece], dst_ref=own_ref.at[piece],
            send_sem=up_send.at[d], recv_sem=up_recv.at[d],
            device_id=(r + 1, c), device_id_type=MESH)

    def down_copy(piece, d):
        return pltpu.make_async_remote_copy(
            src_ref=own_ref.at[piece], dst_ref=own_ref.at[piece],
            send_sem=down_send.at[d], recv_sem=down_recv.at[d],
            device_id=(r - 1, c), device_id_type=MESH)

    def far_copy(piece, slot):
        return pltpu.make_async_remote_copy(
            src_ref=own_ref.at[piece], dst_ref=far_ref.at[piece],
            send_sem=far_send.at[slot], recv_sem=far_recv.at[slot],
            device_id=(r, target), device_id_type=MESH)

    pl.when(r < n - 1)(lambda: up_copy(r, 0).start())
    pl.when(r > 0)(lambda: down_copy(r, 0).start())
    pl.when(r > 0)(lambda: far_copy(r, 0).start())
    for d in range(1, n):
        @pl.when(r >= d)
        def _():
            up_copy(r - d, d - 1).wait_recv()
            pl.when(r < n - 1)(lambda: up_copy(r - d, d).start())
            far_copy(r - d, 2 * d - 1).start()

        @pl.when(r + d < n)
        def _():
            down_copy(r + d, d - 1).wait_recv()

            @pl.when(r > 0)
            def _():
                down_copy(r + d, d).start()
                far_copy(r + d, 2 * d).start()

    @pl.when(r == 0)
    def _():
        far_ref[...] = own_ref[...]

    for d in range(n):
        if d:
            @pl.when(r >= d)
            def _():
                far_copy(r - d, 2 * d - 1).wait()

            @pl.when((r + d < n) & (r > 0))
            def _():
                far_copy(r + d, 2 * d).wait()

            pl.when((r >= d) & (r < n - 1))(lambda: up_copy(r - d, d).wait_send())
            pl.when((r + d < n) & (r > 0))(lambda: down_copy(r + d, d).wait_send())
        else:
            pl.when(r > 0)(lambda: far_copy(r, 0).wait())
            pl.when(r < n - 1)(lambda: up_copy(r, 0).wait_send())
            pl.when(r > 0)(lambda: down_copy(r, 0).wait_send())


def gather_pieces(piece, n):
    shape = jax.ShapeDtypeStruct((n,) + piece.shape, piece.dtype)
    vmem = pl.BlockSpec(memory_space=pltpu.VMEM)
    dma = pltpu.SemaphoreType.DMA
    return pl.pallas_call(
        gather_kernel,
        out_shape=(shape, shape),
        in_specs=[vmem],
        out_specs=(vmem, vmem),
        scratch_shapes=[dma((n,)), dma((n,)), dma((n,)), dma((n,)), dma((2 * n,)), dma((2 * n,))],
        compiler_params=pltpu.CompilerParams(
            collective_id=0, has_side_effects=True, vmem_limit_bytes=VMEM_BYTES),
    )(piece)


def product_kernel(chunk, rows_ref, cols_ref, count_ref, vals_ref, own_ref, far_ref, fwd_ref, tr_ref,
                   x_col, x_row, acc_f, acc_t, loose, packed):
    step, steps = pl.program_id(0), pl.num_programs(0)
    n, _, width = own_ref.shape
    tiles = width // 128
    per_group = 2 * tiles
    nblk = n * GROUPS * per_group
    low = row_iota() < 4
    left = lane_iota() < 64
    keep = low == left
    quarter = lane_iota() // 32
    batch = min(tiles, 16)

    def each_tile(visit):
        def some(i, _):
            q, t0 = i // (tiles // batch), (i % (tiles // batch)) * batch
            for t in range(batch):
                visit(q, t0 + t)
            return 0
        lax.fori_loop(0, n * tiles // batch, some, 0)

    def block_at(q, g, t, parity):
        return q * (GROUPS * per_group) + g * per_group + 2 * t + parity

    def expand(src_ref, dst_ref):
        def tile(q, t):
            s = src_ref[q, :, pl.ds(pl.multiple_of(t * 128, 128), 128)].astype(F32)
            for h in range(2):
                v = s[8 * h:8 * h + 8]
                vl = pltpu.roll(v, 64, 1)
                vs = pltpu.roll(v, 4, 0)
                vls = pltpu.roll(vl, 4, 0)
                dst_ref[block_at(q, 2 * h, t, 0)] = jnp.where(keep, jnp.where(low, v, vls), 0.0)
                dst_ref[block_at(q, 2 * h, t, 1)] = jnp.where(keep, jnp.where(low, vl, vs), 0.0)
                dst_ref[block_at(q, 2 * h + 1, t, 0)] = jnp.where(keep, jnp.where(low, vs, vl), 0.0)
                dst_ref[block_at(q, 2 * h + 1, t, 1)] = jnp.where(keep, jnp.where(low, vls, v), 0.0)
        each_tile(tile)

    part_size = 64

    @pl.when(step == 0)
    def _():
        expand(own_ref, x_col)
        expand(far_ref, x_row)
        spread = spread_matrix()

        def part(i, _):
            at = pl.ds(i * part_size, part_size)
            x = x_row[at].reshape(part_size * 8, 128).astype(BF16)
            x_row[at] = jnp.dot(x, spread, preferred_element_type=F32).reshape(part_size, 8, 128)
            zero = jnp.zeros((part_size, 8, 128), F32)
            acc_f[at] = zero
            acc_t[at] = zero
            return 0
        lax.fori_loop(0, nblk // part_size, part, 0)

    count = count_ref[0]
    first = step * chunk
    live = jnp.clip(count - first, 0, chunk)

    def retile(i, _):
        for s in range(32):
            v = vals_ref[pl.ds(pl.multiple_of(i * 16, 16), 16), s * 128:(s + 1) * 128]
            loose[pl.ds(s, 16, stride=32), :] = v.astype(F32)
        packed[pl.ds(pl.multiple_of(i * 512, 512), 512), :] = loose[...].astype(BF16)
        return 0
    lax.fori_loop(0, (live + 15) // 16, retile, 0)

    def some_slots(i, _):
        for part in range(4):
            at = i * 16 + part * 4
            w = packed[pl.ds(pl.multiple_of(at * 32, 128), 128), :]
            rows, cols, lf, lt = [], [], [], []
            for z in range(4):
                slot = first + at + z
                r, c = rows_ref[slot], cols_ref[slot]
                lf.append(x_col[c])
                lt.append(jnp.where(quarter == z, x_row[r], 0.0))
                used = slot < count
                rows.append(jnp.where(used, r, nblk))
                cols.append(jnp.where(used, c, nblk))
            of = lax.dot_general(jnp.concatenate(lf, 0).astype(BF16), w, (((1,), (1,)), ((), ())),
                                 preferred_element_type=F32)
            ot = jnp.dot(jnp.concatenate(lt, 0).astype(BF16), w, preferred_element_type=F32)
            for z in range(4):
                acc_f[rows[z]] += jnp.where(quarter == z, of[8 * z:8 * z + 8], 0.0)
                acc_t[cols[z]] += ot[8 * z:8 * z + 8]
        return 0
    lax.fori_loop(0, (live + 15) // 16, some_slots, 0)

    @pl.when(step == steps - 1)
    def _():
        spread = spread_matrix()

        def part(i, _):
            at = pl.ds(i * part_size, part_size)
            x = acc_f[at].reshape(part_size * 8, 128)
            hi = x.astype(BF16)
            lo = (x - hi.astype(F32)).astype(BF16)
            back = (((1,), (1,)), ((), ()))
            y = lax.dot_general(hi, spread, back, preferred_element_type=F32)
            y += lax.dot_general(lo, spread, back, preferred_element_type=F32)
            acc_f[at] = y.reshape(part_size, 8, 128)
            return 0
        lax.fori_loop(0, nblk // part_size, part, 0)

        def fold(src_ref, dst_ref):
            def tile(q, t):
                out = []
                for h in range(2):
                    e0, o0 = src_ref[block_at(q, 2 * h, t, 0)], src_ref[block_at(q, 2 * h, t, 1)]
                    e1, o1 = src_ref[block_at(q, 2 * h + 1, t, 0)], src_ref[block_at(q, 2 * h + 1, t, 1)]
                    stay = jnp.where(keep, jnp.where(low, e0, o1), pltpu.roll(jnp.where(low, o0, e1), 64, 1))
                    move = jnp.where(keep, jnp.where(low, e1, o0), pltpu.roll(jnp.where(low, o1, e0), 64, 1))
                    out.append(stay + pltpu.roll(move, 4, 0))
                at = pl.ds(pl.multiple_of(t * 128, 128), 128)
                dst_ref[q, :, at] = jnp.concatenate(out, 0).astype(dst_ref.dtype)
            each_tile(tile)

        fold(acc_f, fwd_ref)
        fold(acc_t, tr_ref)


def block_products(vals, rows, cols, count, own, far):
    slots = rows.shape[0]
    chunk = 128
    n, depth, width = own.shape
    nblk = n * GROUPS * (width // 64)
    whole = pl.BlockSpec((n, depth, width), lambda i, *_: (0, 0, 0))
    return pl.pallas_call(
        functools.partial(product_kernel, chunk),
        out_shape=(jax.ShapeDtypeStruct(own.shape, BF16), jax.ShapeDtypeStruct(own.shape, F32)),
        grid_spec=pltpu.PrefetchScalarGridSpec(
            num_scalar_prefetch=3,
            grid=(slots // chunk,),
            in_specs=[pl.BlockSpec((chunk, vals.shape[1]), lambda i, *_: (i, 0)), whole, whole],
            out_specs=(whole, whole),
            scratch_shapes=[
                pltpu.VMEM((nblk, 8, 128), F32),
                pltpu.VMEM((nblk, 8, 128), F32),
                pltpu.VMEM((nblk + 1, 8, 128), F32),
                pltpu.VMEM((nblk + 1, 8, 128), F32),
                pltpu.VMEM((512, 128), F32),
                pltpu.VMEM((chunk * 32, 128), BF16),
            ],
        ),
        compiler_params=pltpu.CompilerParams(vmem_limit_bytes=VMEM_BYTES),
    )(rows, cols, count, vals, own, far)


def reduce_kernel(fwd_ref, tr_ref, out_ref, far, stage, landed, far_send, far_recv, send, recv):
    n = fwd_ref.shape[0]
    cols = lax.axis_size("col")
    r, c = lax.axis_index("row"), lax.axis_index("col")
    target = lax.rem(c + r, cols)
    source = lax.rem(c - r + cols, cols)
    barrier = pltpu.get_barrier_semaphore()
    for d in range(1, n):
        pl.semaphore_signal(barrier, inc=1, device_id=(lax.rem(r + d, n), c), device_id_type=MESH)

    @pl.when(r > 0)
    def _():
        pl.semaphore_signal(barrier, inc=1, device_id=(r, source), device_id_type=MESH)
    pl.semaphore_wait(barrier, jnp.where(r > 0, n, n - 1))

    def far_copy(d):
        q = lax.rem(r + d, n)
        return pltpu.make_async_remote_copy(
            src_ref=fwd_ref.at[q], dst_ref=far.at[q],
            send_sem=far_send.at[d], recv_sem=far_recv.at[d],
            device_id=(r, target), device_id_type=MESH)

    def row_copy(d):
        return pltpu.make_async_remote_copy(
            src_ref=stage.at[d - 1], dst_ref=landed.at[d - 1],
            send_sem=send.at[d - 1], recv_sem=recv.at[d - 1],
            device_id=(lax.rem(r + d, n), c), device_id_type=MESH)

    order = list(range(1, n)) + [0]

    @pl.when(r > 0)
    def _():
        for d in order:
            far_copy(d).start()

    @pl.when(r == 0)
    def _():
        far[...] = fwd_ref[...]

    for d in order:
        pl.when(r > 0)(lambda: far_copy(d).wait_recv())
        q = lax.rem(r + d, n)
        total = tr_ref[q] + far[q].astype(F32)
        if d:
            stage[d - 1] = total.astype(BF16)
            row_copy(d).start()
    for d in range(1, n):
        row_copy(d).wait_recv()
        total += landed[d - 1].astype(F32)
    width = total.shape[1]
    for g in range(GROUPS):
        out_ref[:, g * width:(g + 1) * width] = total[4 * g:4 * g + 4]
    for d in range(1, n):
        row_copy(d).wait_send()

    @pl.when(r > 0)
    def _():
        for d in order:
            far_copy(d).wait_send()


def reduce_pieces(fwd, tr):
    n, depth, width = fwd.shape
    vmem = pl.BlockSpec(memory_space=pltpu.VMEM)
    dma = pltpu.SemaphoreType.DMA
    return pl.pallas_call(
        reduce_kernel,
        out_shape=jax.ShapeDtypeStruct((depth // GROUPS, GROUPS * width), F32),
        in_specs=[vmem, vmem],
        out_specs=vmem,
        scratch_shapes=[
            pltpu.VMEM((n, depth, width), BF16),
            pltpu.VMEM((n - 1, depth, width), BF16),
            pltpu.VMEM((n - 1, depth, width), BF16),
            dma((n,)), dma((n,)), dma((n - 1,)), dma((n - 1,)),
        ],
        compiler_params=pltpu.CompilerParams(
            collective_id=1, has_side_effects=True, vmem_limit_bytes=VMEM_BYTES),
    )(fwd, tr)


def total_kernel(part_ref, out_ref, slots, send, recv):
    rows, cols = lax.axis_size("row"), lax.axis_size("col")
    count = rows * cols
    r, c = lax.axis_index("row"), lax.axis_index("col")
    me = r * cols + c
    barrier = pltpu.get_barrier_semaphore()

    def peer(d):
        other = lax.rem(me + d, count)
        return (other // cols, lax.rem(other, cols))

    def greet(d, _):
        pl.semaphore_signal(barrier, inc=1, device_id=peer(d), device_id_type=MESH)
        return 0
    lax.fori_loop(1, count, greet, 0)
    slots[me] = part_ref[...]
    pl.semaphore_wait(barrier, count - 1)

    def copy(d):
        return pltpu.make_async_remote_copy(
            src_ref=part_ref, dst_ref=slots.at[me],
            send_sem=send.at[d], recv_sem=recv.at[d],
            device_id=peer(d), device_id_type=MESH)

    def start(d, _):
        copy(d).start()
        return 0

    def finish(d, _):
        copy(d).wait()
        return 0
    lax.fori_loop(1, count, start, 0)
    lax.fori_loop(1, count, finish, 0)
    out_ref[...] = jnp.sum(slots[...], axis=0)


def total_over_devices(part, count):
    vmem = pl.BlockSpec(memory_space=pltpu.VMEM)
    dma = pltpu.SemaphoreType.DMA
    return pl.pallas_call(
        total_kernel,
        out_shape=jax.ShapeDtypeStruct(part.shape, F32),
        in_specs=[vmem],
        out_specs=vmem,
        scratch_shapes=[pltpu.VMEM((count,) + part.shape, F32), dma((count,)), dma((count,))],
        compiler_params=pltpu.CompilerParams(
            collective_id=2, has_side_effects=True, vmem_limit_bytes=VMEM_BYTES),
    )(part)


def body(x_vec, hx_vec, p_vec, hp_vec, theta, precond, tile_vals, tile_rows, tile_cols, tile_count):
    vec_count, piece_len = x_vec.shape
    row_count = lax.axis_size("row")
    col_count = lax.axis_size("col")
    ndim_total = piece_len * row_count * col_count
    residue = (hx_vec - x_vec * theta[:, None]) / precond[None, :]
    width = piece_len // GROUPS
    w_send = residue.astype(BF16).reshape(vec_count, GROUPS, width)
    w_send = jnp.transpose(w_send, (1, 0, 2)).reshape(GROUPS * vec_count, width)
    own, far = gather_pieces(w_send, row_count)
    fwd, tr = block_products(tile_vals[0, 0], tile_rows[0, 0], tile_cols[0, 0], tile_count[0], own, far)
    hw_vec = reduce_pieces(fwd, tr)
    vectors = jnp.concatenate([x_vec, residue, p_vec], 0)
    images = jnp.concatenate([hx_vec, hw_vec, hp_vec], 0)
    dims = (((1,), (1,)), ((), ()))
    local_a = lax.dot_general(vectors, images, dims, precision=lax.Precision.HIGHEST,
                              preferred_element_type=F32)
    local_b = lax.dot_general(vectors, vectors, dims, precision=lax.Precision.HIGHEST,
                              preferred_element_type=F32)
    rows = vectors.shape[0]
    part = jnp.zeros((32, 128), F32).at[:rows, :rows].set(local_a).at[16:16 + rows, :rows].set(local_b)
    total = total_over_devices(part, row_count * col_count) / ndim_total
    return (hw_vec, total[:rows, :rows], total[16:16 + rows, :rows])


def solution(mesh):
    placed = (
        P(None, ("col", "row")),
        P(None, ("col", "row")),
        P(None, ("col", "row")),
        P(None, ("col", "row")),
        P(),
        P(("col", "row")),
        P("row", "col", None, None),
        P("row", "col", None),
        P("row", "col", None),
        P("row", "col"),
    )
    return jax.shard_map(
        body,
        mesh=mesh,
        in_specs=placed,
        out_specs=(P(None, ("col", "row")), P(), P()),
        check_vma=False,
    )
```

```python
import functools
import jax
import jax.numpy as jnp
from jax import lax
from jax.experimental import pallas as pl
from jax.experimental.pallas import tpu as pltpu
from jax.sharding import PartitionSpec as P

BLOCK = 64
GROUPS = 4
MESH = pl.DeviceIdType.MESH
F32 = jnp.float32
BF16 = jnp.bfloat16
VMEM_BYTES = 58 * 1024 * 1024


def row_iota():
    return lax.broadcasted_iota(jnp.int32, (8, 128), 0)


def lane_iota():
    return lax.broadcasted_iota(jnp.int32, (8, 128), 1)


def spread_matrix():
    a = lax.broadcasted_iota(jnp.int32, (128, 128), 0)
    b = lax.broadcasted_iota(jnp.int32, (128, 128), 1)
    return jnp.where((a % 64) == 2 * (b % 32) + a // 64, 1.0, 0.0).astype(BF16)


def gather_kernel(w_ref, own_ref, far_ref, up_send, up_recv, down_send, down_recv, far_send, far_recv):
    n = own_ref.shape[0]
    cols = lax.axis_size("col")
    r, c = lax.axis_index("row"), lax.axis_index("col")
    source = lax.rem(c + r, cols)
    target = lax.rem(c - r + cols, cols)
    barrier = pltpu.get_barrier_semaphore()

    def greet(row, col):
        pl.semaphore_signal(barrier, inc=1, device_id=(row, col), device_id_type=MESH)

    pl.when(r > 0)(lambda: greet(r - 1, c))
    pl.when(r < n - 1)(lambda: greet(r + 1, c))
    pl.when(r > 0)(lambda: greet(r, source))
    own_ref[r] = w_ref[...]
    pl.semaphore_wait(barrier, jnp.where(r > 0, jnp.where(r < n - 1, 3, 2), 1))

    def up_copy(piece, d):
        return pltpu.make_async_remote_copy(
            src_ref=own_ref.at[piece], dst_ref=own_ref.at[piece],
            send_sem=up_send.at[d], recv_sem=up_recv.at[d],
            device_id=(r + 1, c), device_id_type=MESH)

    def down_copy(piece, d):
        return pltpu.make_async_remote_copy(
            src_ref=own_ref.at[piece], dst_ref=own_ref.at[piece],
            send_sem=down_send.at[d], recv_sem=down_recv.at[d],
            device_id=(r - 1, c), device_id_type=MESH)

    def far_copy(piece, slot):
        return pltpu.make_async_remote_copy(
            src_ref=own_ref.at[piece], dst_ref=far_ref.at[piece],
            send_sem=far_send.at[slot], recv_sem=far_recv.at[slot],
            device_id=(r, target), device_id_type=MESH)

    pl.when(r < n - 1)(lambda: up_copy(r, 0).start())
    pl.when(r > 0)(lambda: down_copy(r, 0).start())
    pl.when(r > 0)(lambda: far_copy(r, 0).start())
    for d in range(1, n):
        @pl.when(r >= d)
        def _():
            up_copy(r - d, d - 1).wait_recv()
            pl.when(r < n - 1)(lambda: up_copy(r - d, d).start())
            far_copy(r - d, 2 * d - 1).start()

        @pl.when(r + d < n)
        def _():
            down_copy(r + d, d - 1).wait_recv()

            @pl.when(r > 0)
            def _():
                down_copy(r + d, d).start()
                far_copy(r + d, 2 * d).start()

    @pl.when(r == 0)
    def _():
        far_ref[...] = own_ref[...]

    for d in range(n):
        if d:
            @pl.when(r >= d)
            def _():
                far_copy(r - d, 2 * d - 1).wait()

            @pl.when((r + d < n) & (r > 0))
            def _():
                far_copy(r + d, 2 * d).wait()

            pl.when((r >= d) & (r < n - 1))(lambda: up_copy(r - d, d).wait_send())
            pl.when((r + d < n) & (r > 0))(lambda: down_copy(r + d, d).wait_send())
        else:
            pl.when(r > 0)(lambda: far_copy(r, 0).wait())
            pl.when(r < n - 1)(lambda: up_copy(r, 0).wait_send())
            pl.when(r > 0)(lambda: down_copy(r, 0).wait_send())


def gather_pieces(piece, n):
    shape = jax.ShapeDtypeStruct((n,) + piece.shape, piece.dtype)
    vmem = pl.BlockSpec(memory_space=pltpu.VMEM)
    dma = pltpu.SemaphoreType.DMA
    return pl.pallas_call(
        gather_kernel,
        out_shape=(shape, shape),
        in_specs=[vmem],
        out_specs=(vmem, vmem),
        scratch_shapes=[dma((n,)), dma((n,)), dma((n,)), dma((n,)), dma((2 * n,)), dma((2 * n,))],
        compiler_params=pltpu.CompilerParams(
            collective_id=0, has_side_effects=True, vmem_limit_bytes=VMEM_BYTES),
    )(piece)


def product_kernel(chunk, rows_ref, cols_ref, count_ref, vals_ref, own_ref, far_ref, fwd_ref, tr_ref,
                   x_col, x_row, acc_f, acc_t, loose, packed):
    step, steps = pl.program_id(0), pl.num_programs(0)
    n, _, width = own_ref.shape
    tiles = width // 128
    per_group = 2 * tiles
    nblk = n * GROUPS * per_group
    low = row_iota() < 4
    left = lane_iota() < 64
    keep = low == left
    quarter = lane_iota() // 32
    batch = min(tiles, 16)

    def each_tile(visit):
        def some(i, _):
            q, t0 = i // (tiles // batch), (i % (tiles // batch)) * batch
            for t in range(batch):
                visit(q, t0 + t)
            return 0
        lax.fori_loop(0, n * tiles // batch, some, 0)

    def block_at(q, g, t, parity):
        return q * (GROUPS * per_group) + g * per_group + 2 * t + parity

    def expand(src_ref, dst_ref):
        def tile(q, t):
            s = src_ref[q, :, pl.ds(pl.multiple_of(t * 128, 128), 128)].astype(F32)
            for h in range(2):
                v = s[8 * h:8 * h + 8]
                vl = pltpu.roll(v, 64, 1)
                vs = pltpu.roll(v, 4, 0)
                vls = pltpu.roll(vl, 4, 0)
                dst_ref[block_at(q, 2 * h, t, 0)] = jnp.where(keep, jnp.where(low, v, vls), 0.0)
                dst_ref[block_at(q, 2 * h, t, 1)] = jnp.where(keep, jnp.where(low, vl, vs), 0.0)
                dst_ref[block_at(q, 2 * h + 1, t, 0)] = jnp.where(keep, jnp.where(low, vs, vl), 0.0)
                dst_ref[block_at(q, 2 * h + 1, t, 1)] = jnp.where(keep, jnp.where(low, vls, v), 0.0)
        each_tile(tile)

    part_size = 64

    @pl.when(step == 0)
    def _():
        expand(own_ref, x_col)
        expand(far_ref, x_row)
        spread = spread_matrix()

        def part(i, _):
            at = pl.ds(i * part_size, part_size)
            x = x_row[at].reshape(part_size * 8, 128).astype(BF16)
            x_row[at] = jnp.dot(x, spread, preferred_element_type=F32).reshape(part_size, 8, 128)
            zero = jnp.zeros((part_size, 8, 128), F32)
            acc_f[at] = zero
            acc_t[at] = zero
            return 0
        lax.fori_loop(0, nblk // part_size, part, 0)

    count = count_ref[0]
    first = step * chunk
    live = jnp.clip(count - first, 0, chunk)

    def retile(i, _):
        for s in range(32):
            v = vals_ref[pl.ds(pl.multiple_of(i * 16, 16), 16), s * 128:(s + 1) * 128]
            loose[pl.ds(s, 16, stride=32), :] = v.astype(F32)
        packed[pl.ds(pl.multiple_of(i * 512, 512), 512), :] = loose[...].astype(BF16)
        return 0
    lax.fori_loop(0, (live + 15) // 16, retile, 0)

    def some_slots(i, _):
        for part in range(4):
            at = i * 16 + part * 4
            w = packed[pl.ds(pl.multiple_of(at * 32, 128), 128), :]
            rows, cols, lf, lt = [], [], [], []
            for z in range(4):
                slot = first + at + z
                r, c = rows_ref[slot], cols_ref[slot]
                lf.append(x_col[c])
                lt.append(jnp.where(quarter == z, x_row[r], 0.0))
                used = slot < count
                rows.append(jnp.where(used, r, nblk))
                cols.append(jnp.where(used, c, nblk))
            of = lax.dot_general(jnp.concatenate(lf, 0).astype(BF16), w, (((1,), (1,)), ((), ())),
                                 preferred_element_type=F32)
            ot = jnp.dot(jnp.concatenate(lt, 0).astype(BF16), w, preferred_element_type=F32)
            for z in range(4):
                acc_f[rows[z]] += jnp.where(quarter == z, of[8 * z:8 * z + 8], 0.0)
                acc_t[cols[z]] += ot[8 * z:8 * z + 8]
        return 0
    lax.fori_loop(0, (live + 15) // 16, some_slots, 0)

    @pl.when(step == steps - 1)
    def _():
        spread = spread_matrix()

        def part(i, _):
            at = pl.ds(i * part_size, part_size)
            x = acc_f[at].reshape(part_size * 8, 128)
            hi = x.astype(BF16)
            lo = (x - hi.astype(F32)).astype(BF16)
            back = (((1,), (1,)), ((), ()))
            y = lax.dot_general(hi, spread, back, preferred_element_type=F32)
            y += lax.dot_general(lo, spread, back, preferred_element_type=F32)
            acc_f[at] = y.reshape(part_size, 8, 128)
            return 0
        lax.fori_loop(0, nblk // part_size, part, 0)

        def fold(src_ref, dst_ref):
            def tile(q, t):
                out = []
                for h in range(2):
                    e0, o0 = src_ref[block_at(q, 2 * h, t, 0)], src_ref[block_at(q, 2 * h, t, 1)]
                    e1, o1 = src_ref[block_at(q, 2 * h + 1, t, 0)], src_ref[block_at(q, 2 * h + 1, t, 1)]
                    stay = jnp.where(keep, jnp.where(low, e0, o1), pltpu.roll(jnp.where(low, o0, e1), 64, 1))
                    move = jnp.where(keep, jnp.where(low, e1, o0), pltpu.roll(jnp.where(low, o1, e0), 64, 1))
                    out.append(stay + pltpu.roll(move, 4, 0))
                at = pl.ds(pl.multiple_of(t * 128, 128), 128)
                dst_ref[q, :, at] = jnp.concatenate(out, 0).astype(dst_ref.dtype)
            each_tile(tile)

        fold(acc_f, fwd_ref)
        fold(acc_t, tr_ref)


def block_products(vals, rows, cols, count, own, far):
    slots = rows.shape[0]
    chunk = 128
    n, depth, width = own.shape
    nblk = n * GROUPS * (width // 64)
    whole = pl.BlockSpec((n, depth, width), lambda i, *_: (0, 0, 0))
    return pl.pallas_call(
        functools.partial(product_kernel, chunk),
        out_shape=(jax.ShapeDtypeStruct(own.shape, BF16), jax.ShapeDtypeStruct(own.shape, F32)),
        grid_spec=pltpu.PrefetchScalarGridSpec(
            num_scalar_prefetch=3,
            grid=(slots // chunk,),
            in_specs=[pl.BlockSpec((chunk, vals.shape[1]), lambda i, *_: (i, 0)), whole, whole],
            out_specs=(whole, whole),
            scratch_shapes=[
                pltpu.VMEM((nblk, 8, 128), F32),
                pltpu.VMEM((nblk, 8, 128), F32),
                pltpu.VMEM((nblk + 1, 8, 128), F32),
                pltpu.VMEM((nblk + 1, 8, 128), F32),
                pltpu.VMEM((512, 128), F32),
                pltpu.VMEM((chunk * 32, 128), BF16),
            ],
        ),
        compiler_params=pltpu.CompilerParams(vmem_limit_bytes=VMEM_BYTES),
    )(rows, cols, count, vals, own, far)


def reduce_kernel(fwd_ref, tr_ref, x_ref, res_ref, p_ref, hx_ref, hp_ref, out_ref, a_ref, b_ref,
                  far, stage, landed, part, half, col_slots, row_slots,
                  far_send, far_recv, send, recv, col_send, col_recv, row_send, row_recv):
    n = fwd_ref.shape[0]
    vecs, length = x_ref.shape
    basis = 3 * vecs
    cols = lax.axis_size("col")
    r, c = lax.axis_index("row"), lax.axis_index("col")
    target = lax.rem(c + r, cols)
    barrier = pltpu.get_barrier_semaphore()
    for d in range(1, n):
        pl.semaphore_signal(barrier, inc=1, device_id=(lax.rem(r + d, n), c), device_id_type=MESH)
    for d in range(1, cols):
        pl.semaphore_signal(barrier, inc=1, device_id=(r, lax.rem(c + d, cols)), device_id_type=MESH)
    pl.semaphore_wait(barrier, n + cols - 2)

    def far_copy(d):
        q = lax.rem(r + d, n)
        return pltpu.make_async_remote_copy(
            src_ref=fwd_ref.at[q], dst_ref=far.at[q],
            send_sem=far_send.at[d], recv_sem=far_recv.at[d],
            device_id=(r, target), device_id_type=MESH)

    def row_copy(d):
        return pltpu.make_async_remote_copy(
            src_ref=stage.at[d - 1], dst_ref=landed.at[d - 1],
            send_sem=send.at[d - 1], recv_sem=recv.at[d - 1],
            device_id=(lax.rem(r + d, n), c), device_id_type=MESH)

    def col_sum_copy(d):
        return pltpu.make_async_remote_copy(
            src_ref=part, dst_ref=col_slots.at[c],
            send_sem=col_send.at[d], recv_sem=col_recv.at[d],
            device_id=(r, lax.rem(c + d, cols)), device_id_type=MESH)

    def row_sum_copy(d):
        return pltpu.make_async_remote_copy(
            src_ref=half, dst_ref=row_slots.at[r],
            send_sem=row_send.at[d], recv_sem=row_recv.at[d],
            device_id=(lax.rem(r + d, n), c), device_id_type=MESH)

    def products(left_refs, right_refs):
        span = min(length, 2048)
        height = len(left_refs) * vecs
        across = len(right_refs) * vecs

        def some(i, total):
            at = pl.ds(pl.multiple_of(i * span, span), span)
            v = jnp.concatenate([ref[:, at] for ref in left_refs], 0)
            w = jnp.concatenate([ref[:, at] for ref in right_refs], 0)
            return total + lax.dot_general(v, w, (((1,), (1,)), ((), ())), precision=lax.Precision.HIGHEST,
                                           preferred_element_type=F32)
        return lax.fori_loop(0, length // span, some, jnp.zeros((height, across), F32))

    order = list(range(1, n)) + [0]

    @pl.when(r > 0)
    def _():
        for d in order:
            far_copy(d).start()

    @pl.when(r == 0)
    def _():
        far[...] = fwd_ref[...]

    part[...] = jnp.zeros_like(part)
    left = [x_ref, res_ref, p_ref]
    part[:basis, :5 * vecs] = products(left, left + [hx_ref, hp_ref])

    for d in order:
        pl.when(r > 0)(lambda: far_copy(d).wait_recv())
        q = lax.rem(r + d, n)
        total = tr_ref[q] + far[q].astype(F32)
        if d:
            stage[d - 1] = total.astype(BF16)
            row_copy(d).start()
    for d in range(1, n):
        row_copy(d).wait_recv()
        total += landed[d - 1].astype(F32)
    width = total.shape[1]
    for g in range(GROUPS):
        out_ref[:, g * width:(g + 1) * width] = total[4 * g:4 * g + 4]

    part[:basis, 5 * vecs:6 * vecs] = products(left, [out_ref])
    for d in range(1, cols):
        col_sum_copy(d).start()
    col_slots[c] = part[...]
    for d in range(1, cols):
        col_sum_copy(d).wait_recv()
    half[...] = jnp.sum(col_slots[...], axis=0)
    for d in range(1, n):
        row_sum_copy(d).start()
    row_slots[r] = half[...]
    for d in range(1, n):
        row_sum_copy(d).wait_recv()
    gram = jnp.sum(row_slots[...], axis=0) * (1.0 / (length * n * cols))
    b_ref[...] = gram[:basis, :basis]
    a_ref[:, :vecs] = gram[:basis, 3 * vecs:4 * vecs]
    a_ref[:, vecs:2 * vecs] = gram[:basis, 5 * vecs:6 * vecs]
    a_ref[:, 2 * vecs:] = gram[:basis, 4 * vecs:5 * vecs]

    for d in range(1, n):
        row_copy(d).wait_send()
        row_sum_copy(d).wait_send()
    for d in range(1, cols):
        col_sum_copy(d).wait_send()

    @pl.when(r > 0)
    def _():
        for d in order:
            far_copy(d).wait_send()


def reduce_pieces(fwd, tr, x_vec, residue, p_vec, hx_vec, hp_vec, cols):
    n, depth, width = fwd.shape
    basis = 3 * x_vec.shape[0]
    vmem = pl.BlockSpec(memory_space=pltpu.VMEM)
    dma = pltpu.SemaphoreType.DMA
    small = (16, 128)
    gram = jax.ShapeDtypeStruct((basis, basis), F32)
    return pl.pallas_call(
        reduce_kernel,
        out_shape=(jax.ShapeDtypeStruct(x_vec.shape, F32), gram, gram),
        in_specs=[vmem] * 7,
        out_specs=(vmem,) * 3,
        scratch_shapes=[
            pltpu.VMEM((n, depth, width), BF16),
            pltpu.VMEM((n - 1, depth, width), BF16),
            pltpu.VMEM((n - 1, depth, width), BF16),
            pltpu.VMEM(small, F32),
            pltpu.VMEM(small, F32),
            pltpu.VMEM((cols,) + small, F32),
            pltpu.VMEM((n,) + small, F32),
            dma((n,)), dma((n,)), dma((n - 1,)), dma((n - 1,)),
            dma((cols,)), dma((cols,)), dma((n,)), dma((n,)),
        ],
        compiler_params=pltpu.CompilerParams(
            collective_id=1, has_side_effects=True, vmem_limit_bytes=VMEM_BYTES),
    )(fwd, tr, x_vec, residue, p_vec, hx_vec, hp_vec)


def body(x_vec, hx_vec, p_vec, hp_vec, theta, precond, tile_vals, tile_rows, tile_cols, tile_count):
    vec_count, piece_len = x_vec.shape
    row_count = lax.axis_size("row")
    col_count = lax.axis_size("col")
    residue = (hx_vec - x_vec * theta[:, None]) / precond[None, :]
    width = piece_len // GROUPS
    w_send = residue.astype(BF16).reshape(vec_count, GROUPS, width)
    w_send = jnp.transpose(w_send, (1, 0, 2)).reshape(GROUPS * vec_count, width)
    own, far = gather_pieces(w_send, row_count)
    fwd, tr = block_products(tile_vals[0, 0], tile_rows[0, 0], tile_cols[0, 0], tile_count[0], own, far)
    return reduce_pieces(fwd, tr, x_vec, residue, p_vec, hx_vec, hp_vec, col_count)


def solution(mesh):
    placed = (
        P(None, ("col", "row")),
        P(None, ("col", "row")),
        P(None, ("col", "row")),
        P(None, ("col", "row")),
        P(),
        P(("col", "row")),
        P("row", "col", None, None),
        P("row", "col", None),
        P("row", "col", None),
        P("row", "col"),
    )
    return jax.shard_map(
        body,
        mesh=mesh,
        in_specs=placed,
        out_specs=(P(None, ("col", "row")), P(), P()),
        check_vma=False,
    )
```

```python
import functools
import jax
import jax.numpy as jnp
from jax import lax
from jax.experimental import pallas as pl
from jax.experimental.pallas import tpu as pltpu
from jax.sharding import PartitionSpec as P

BLOCK = 64
GROUPS = 4
CHUNK = 128
TOGETHER = 32
PART = 64
SMALL = (24, 128)
MESH = pl.DeviceIdType.MESH
F32 = jnp.float32
BF16 = jnp.bfloat16
VMEM_BYTES = 58 * 1024 * 1024


def row_iota():
    return lax.broadcasted_iota(jnp.int32, (8, 128), 0)


def lane_iota():
    return lax.broadcasted_iota(jnp.int32, (8, 128), 1)


def spread_matrix():
    a = lax.broadcasted_iota(jnp.int32, (128, 128), 0)
    b = lax.broadcasted_iota(jnp.int32, (128, 128), 1)
    return jnp.where((a % 64) == 2 * (b % 32) + a // 64, 1.0, 0.0).astype(BF16)


def gather_kernel(x_ref, hx_ref, p_ref, hp_ref, theta_ref, precond_ref, own_ref, res_ref, gram_ref,
                  up_send, up_recv, down_send, down_recv):
    n, _, width = own_ref.shape
    vecs, length = x_ref.shape
    r, c = lax.axis_index("row"), lax.axis_index("col")
    barrier = pltpu.get_barrier_semaphore()

    def greet(row):
        pl.semaphore_signal(barrier, inc=1, device_id=(row, c), device_id_type=MESH)

    pl.when(r > 0)(lambda: greet(r - 1))
    pl.when(r < n - 1)(lambda: greet(r + 1))
    which = lax.broadcasted_iota(jnp.int32, (vecs, 1), 0)
    theta = jnp.zeros((vecs, 1), F32)
    for k in range(vecs):
        theta = jnp.where(which == k, theta_ref[k], theta)
    for g in range(GROUPS):
        at = slice(g * width, (g + 1) * width)
        res_ref[:, at] = (hx_ref[:, at] - x_ref[:, at] * theta) / precond_ref[:, at]
    own_ref[r] = jnp.concatenate(
        [res_ref[:, g * width:(g + 1) * width] for g in range(GROUPS)], 0).astype(BF16)
    pl.semaphore_wait(barrier, jnp.where((r > 0) & (r < n - 1), 2, 1))

    def up_copy(piece, d):
        return pltpu.make_async_remote_copy(
            src_ref=own_ref.at[piece], dst_ref=own_ref.at[piece],
            send_sem=up_send.at[d], recv_sem=up_recv.at[d],
            device_id=(r + 1, c), device_id_type=MESH)

    def down_copy(piece, d):
        return pltpu.make_async_remote_copy(
            src_ref=own_ref.at[piece], dst_ref=own_ref.at[piece],
            send_sem=down_send.at[d], recv_sem=down_recv.at[d],
            device_id=(r - 1, c), device_id_type=MESH)

    span = min(length, 2048)
    spans = length // span
    each = -(-spans // (n - 1))
    left = [x_ref, res_ref, p_ref]
    right = left + [hx_ref, hp_ref]

    def some(i, total):
        at = pl.ds(pl.multiple_of(i * span, span), span)
        v = jnp.concatenate([ref[:, at] for ref in left], 0)
        w = jnp.concatenate([ref[:, at] for ref in right], 0)
        return total + lax.dot_general(v, w, (((1,), (1,)), ((), ())), precision=lax.Precision.HIGHEST,
                                       preferred_element_type=F32)

    pl.when(r < n - 1)(lambda: up_copy(r, 0).start())
    pl.when(r > 0)(lambda: down_copy(r, 0).start())
    gram = jnp.zeros((3 * vecs, 5 * vecs), F32)
    for d in range(1, n):
        gram = lax.fori_loop(min((d - 1) * each, spans), min(d * each, spans), some, gram)

        @pl.when(r >= d)
        def _():
            up_copy(r - d, d - 1).wait_recv()
            pl.when(r < n - 1)(lambda: up_copy(r - d, d).start())

        @pl.when(r + d < n)
        def _():
            down_copy(r + d, d - 1).wait_recv()
            pl.when(r > 0)(lambda: down_copy(r + d, d).start())

    gram_ref[...] = jnp.zeros_like(gram_ref)
    gram_ref[:3 * vecs, :5 * vecs] = gram
    for d in range(n):
        pl.when((r >= d) & (r < n - 1))(lambda: up_copy(r - d, d).wait_send())
        pl.when((r + d < n) & (r > 0))(lambda: down_copy(r + d, d).wait_send())


def gather_pieces(x_vec, hx_vec, p_vec, hp_vec, theta, precond, n):
    vecs, length = x_vec.shape
    vmem = pl.BlockSpec(memory_space=pltpu.VMEM)
    dma = pltpu.SemaphoreType.DMA
    return pl.pallas_call(
        gather_kernel,
        out_shape=(
            jax.ShapeDtypeStruct((n, GROUPS * vecs, length // GROUPS), BF16),
            jax.ShapeDtypeStruct(x_vec.shape, F32),
            jax.ShapeDtypeStruct(SMALL, F32),
        ),
        in_specs=[vmem] * 4 + [pl.BlockSpec(memory_space=pltpu.SMEM), vmem],
        out_specs=(vmem,) * 3,
        scratch_shapes=[dma((n,)), dma((n,)), dma((n,)), dma((n,))],
        compiler_params=pltpu.CompilerParams(
            collective_id=0, has_side_effects=True, vmem_limit_bytes=VMEM_BYTES),
    )(x_vec, hx_vec, p_vec, hp_vec, theta, precond.reshape(1, length))


def block_at(shape, q, g, t, parity):
    per_group = 2 * (shape[2] // 128)
    return q * (GROUPS * per_group) + g * per_group + 2 * t + parity


def each_tile(shape, visit):
    n, tiles = shape[0], shape[2] // 128
    batch = min(tiles, 16)

    def some(i, _):
        q, t0 = i // (tiles // batch), (i % (tiles // batch)) * batch
        for t in range(batch):
            visit(q, t0 + t)
        return 0
    lax.fori_loop(0, n * tiles // batch, some, 0)


def expand(src_ref, dst_ref):
    low = row_iota() < 4
    keep = low == (lane_iota() < 64)
    shape = src_ref.shape

    def tile(q, t):
        s = src_ref[q, :, pl.ds(pl.multiple_of(t * 128, 128), 128)].astype(F32)
        for h in range(2):
            v = s[8 * h:8 * h + 8]
            vl = pltpu.roll(v, 64, 1)
            vs = pltpu.roll(v, 4, 0)
            vls = pltpu.roll(vl, 4, 0)
            g = 2 * h
            dst_ref[block_at(shape, q, g, t, 0)] = jnp.where(keep, jnp.where(low, v, vls), 0.0)
            dst_ref[block_at(shape, q, g, t, 1)] = jnp.where(keep, jnp.where(low, vl, vs), 0.0)
            dst_ref[block_at(shape, q, g + 1, t, 0)] = jnp.where(keep, jnp.where(low, vs, vl), 0.0)
            dst_ref[block_at(shape, q, g + 1, t, 1)] = jnp.where(keep, jnp.where(low, vls, v), 0.0)
    each_tile(shape, tile)


def fold(src_ref, dst_ref):
    low = row_iota() < 4
    keep = low == (lane_iota() < 64)
    shape = dst_ref.shape

    def tile(q, t):
        out = []
        for h in range(2):
            e0, o0, e1, o1 = [src_ref[block_at(shape, q, 2 * h + i // 2, t, i % 2)] for i in range(4)]
            stay = jnp.where(keep, jnp.where(low, e0, o1), pltpu.roll(jnp.where(low, o0, e1), 64, 1))
            move = jnp.where(keep, jnp.where(low, e1, o0), pltpu.roll(jnp.where(low, o1, e0), 64, 1))
            out.append(stay + pltpu.roll(move, 4, 0))
        at = pl.ds(pl.multiple_of(t * 128, 128), 128)
        dst_ref[q, :, at] = jnp.concatenate(out, 0).astype(dst_ref.dtype)
    each_tile(shape, tile)


def each_part(blocks, visit):
    def part(i, _):
        visit(pl.ds(i * PART, PART))
        return 0
    lax.fori_loop(0, blocks // PART, part, 0)


def forward_kernel(rows_ref, cols_ref, count_ref, vals_ref, own_ref, packed, fwd_ref, x_col, acc, loose):
    step, steps = pl.program_id(0), pl.num_programs(0)
    nblk = x_col.shape[0]
    quarter = lane_iota() // 32

    @pl.when(step == 0)
    def _():
        expand(own_ref, x_col)

        def clear(at):
            acc[at] = jnp.zeros((PART, 8, 128), F32)
        each_part(nblk, clear)

    count = count_ref[0]
    first = step * CHUNK
    live = jnp.clip(count - first, 0, CHUNK)

    def some_slots(i, _):
        base = i * TOGETHER
        for half in range(TOGETHER // 16):
            z0 = pl.multiple_of(base + half * 16, 16)
            for s in range(32):
                v = vals_ref[pl.ds(z0, 16), s * 128:(s + 1) * 128]
                loose[half, pl.ds(s, 16, stride=32), :] = v.astype(F32)
        for part in range(TOGETHER // 4):
            at = base + part * 4
            w = loose[part // 4, (part % 4) * 128:(part % 4 + 1) * 128, :].astype(BF16)
            packed[pl.ds(pl.multiple_of(at * 32, 128), 128), :] = w
            rows, lf = [], []
            for z in range(4):
                slot = first + at + z
                lf.append(x_col[cols_ref[slot]])
                rows.append(jnp.where(slot < count, rows_ref[slot], nblk))
            of = lax.dot_general(jnp.concatenate(lf, 0).astype(BF16), w, (((1,), (1,)), ((), ())),
                                 preferred_element_type=F32)
            for z in range(4):
                acc[rows[z]] += jnp.where(quarter == z, of[8 * z:8 * z + 8], 0.0)
        return 0
    lax.fori_loop(0, (live + TOGETHER - 1) // TOGETHER, some_slots, 0)

    @pl.when(step == steps - 1)
    def _():
        spread = spread_matrix()

        def part(at):
            x = acc[at].reshape(PART * 8, 128)
            hi = x.astype(BF16)
            lo = (x - hi.astype(F32)).astype(BF16)
            back = (((1,), (1,)), ((), ()))
            y = lax.dot_general(hi, spread, back, preferred_element_type=F32)
            y += lax.dot_general(lo, spread, back, preferred_element_type=F32)
            acc[at] = y.reshape(PART, 8, 128)
        each_part(nblk, part)
        fold(acc, fwd_ref)


def transposed_kernel(rows_ref, cols_ref, count_ref, packed, far_ref, tr_ref, x_row, acc):
    step, steps = pl.program_id(0), pl.num_programs(0)
    nblk = x_row.shape[0]
    quarter = lane_iota() // 32

    @pl.when(step == 0)
    def _():
        expand(far_ref, x_row)
        spread = spread_matrix()

        def part(at):
            x = x_row[at].reshape(PART * 8, 128).astype(BF16)
            x_row[at] = jnp.dot(x, spread, preferred_element_type=F32).reshape(PART, 8, 128)
            acc[at] = jnp.zeros((PART, 8, 128), F32)
        each_part(nblk, part)

    count = count_ref[0]
    first = step * CHUNK
    live = jnp.clip(count - first, 0, CHUNK)

    def some_slots(i, _):
        for part in range(TOGETHER // 4):
            at = i * TOGETHER + part * 4
            w = packed[pl.ds(pl.multiple_of(at * 32, 128), 128), :]
            cols, lt = [], []
            for z in range(4):
                slot = first + at + z
                lt.append(jnp.where(quarter == z, x_row[rows_ref[slot]], 0.0))
                cols.append(jnp.where(slot < count, cols_ref[slot], nblk))
            ot = jnp.dot(jnp.concatenate(lt, 0).astype(BF16), w, preferred_element_type=F32)
            for z in range(4):
                acc[cols[z]] += ot[8 * z:8 * z + 8]
        return 0
    lax.fori_loop(0, (live + TOGETHER - 1) // TOGETHER, some_slots, 0)

    pl.when(step == steps - 1)(lambda: fold(acc, tr_ref))


def cost(slots):
    return pl.CostEstimate(flops=slots * 4 * 128 * 128 * 64, bytes_accessed=slots * 16384, transcendentals=0)


def forward_products(vals, rows, cols, count, own):
    slots, size = vals.shape
    n, depth, width = own.shape
    nblk = n * GROUPS * (width // 64)
    whole = pl.BlockSpec((n, depth, width), lambda i, *_: (0, 0, 0))
    tall = CHUNK * size // 128
    return pl.pallas_call(
        forward_kernel,
        out_shape=(jax.ShapeDtypeStruct((slots * size // 128, 128), BF16), jax.ShapeDtypeStruct(own.shape, BF16)),
        grid_spec=pltpu.PrefetchScalarGridSpec(
            num_scalar_prefetch=3,
            grid=(slots // CHUNK,),
            in_specs=[pl.BlockSpec((CHUNK, size), lambda i, *_: (i, 0)), whole],
            out_specs=(pl.BlockSpec((tall, 128), lambda i, *_: (i, 0)), whole),
            scratch_shapes=[
                pltpu.VMEM((nblk, 8, 128), F32),
                pltpu.VMEM((nblk + 1, 8, 128), F32),
                pltpu.VMEM((TOGETHER // 16, 512, 128), F32),
            ],
        ),
        cost_estimate=cost(slots),
        compiler_params=pltpu.CompilerParams(vmem_limit_bytes=VMEM_BYTES),
    )(rows, cols, count, vals, own)


def transposed_products(packed, rows, cols, count, far):
    slots = rows.shape[0]
    n, depth, width = far.shape
    nblk = n * GROUPS * (width // 64)
    whole = pl.BlockSpec((n, depth, width), lambda i, *_: (0, 0, 0))
    tall = CHUNK * packed.shape[0] // slots
    return pl.pallas_call(
        transposed_kernel,
        out_shape=jax.ShapeDtypeStruct(far.shape, F32),
        grid_spec=pltpu.PrefetchScalarGridSpec(
            num_scalar_prefetch=3,
            grid=(slots // CHUNK,),
            in_specs=[pl.BlockSpec((tall, 128), lambda i, *_: (i, 0)), whole],
            out_specs=whole,
            scratch_shapes=[
                pltpu.VMEM((nblk, 8, 128), F32),
                pltpu.VMEM((nblk + 1, 8, 128), F32),
            ],
        ),
        cost_estimate=cost(slots),
        compiler_params=pltpu.CompilerParams(vmem_limit_bytes=VMEM_BYTES),
    )(rows, cols, count, packed, far)


def reduce_kernel(came_ref, tr_ref, x_ref, res_ref, p_ref, gram_ref, out_ref, sum_ref,
                  stage, landed, part, half, col_slots, row_slots,
                  send, recv, col_send, col_recv, row_send, row_recv):
    n, _, width = came_ref.shape
    vecs, length = x_ref.shape
    cols = lax.axis_size("col")
    r, c = lax.axis_index("row"), lax.axis_index("col")
    barrier = pltpu.get_barrier_semaphore()
    for d in range(1, n):
        pl.semaphore_signal(barrier, inc=1, device_id=(lax.rem(r + d, n), c), device_id_type=MESH)
    for d in range(1, cols):
        pl.semaphore_signal(barrier, inc=1, device_id=(r, lax.rem(c + d, cols)), device_id_type=MESH)

    def row_copy(d):
        return pltpu.make_async_remote_copy(
            src_ref=stage.at[d - 1], dst_ref=landed.at[d - 1],
            send_sem=send.at[d - 1], recv_sem=recv.at[d - 1],
            device_id=(lax.rem(r + d, n), c), device_id_type=MESH)

    def col_sum_copy(d):
        return pltpu.make_async_remote_copy(
            src_ref=part, dst_ref=col_slots.at[c],
            send_sem=col_send.at[d], recv_sem=col_recv.at[d],
            device_id=(r, lax.rem(c + d, cols)), device_id_type=MESH)

    def row_sum_copy(d):
        return pltpu.make_async_remote_copy(
            src_ref=half, dst_ref=row_slots.at[r],
            send_sem=row_send.at[d], recv_sem=row_recv.at[d],
            device_id=(lax.rem(r + d, n), c), device_id_type=MESH)

    def summed(d):
        q = lax.rem(r + d, n)
        return tr_ref[q] + came_ref[q].astype(F32)

    for d in range(1, n):
        stage[d - 1] = summed(d).astype(BF16)
        if d == 1:
            pl.semaphore_wait(barrier, n + cols - 2)
        row_copy(d).start()
    part[...] = gram_ref[...]
    total = summed(0)
    for d in range(1, n):
        row_copy(d).wait_recv()
        total += landed[d - 1].astype(F32)
    for g in range(GROUPS):
        out_ref[:, g * width:(g + 1) * width] = total[4 * g:4 * g + 4]

    def dots(i, sums):
        sums = list(sums)
        for t in range(8):
            at = pl.ds(pl.multiple_of((i * 8 + t) * 128, 128), 128)
            hw = out_ref[:, at]
            for v in range(3 * vecs):
                row = (x_ref, res_ref, p_ref)[v // vecs][v % vecs:v % vecs + 1, at]
                sums[v] = sums[v] + row * hw
        return tuple(sums)

    sums = lax.fori_loop(0, length // 1024, dots, tuple(jnp.zeros((vecs, 128), F32) for _ in range(3 * vecs)))
    for v in range(3 * vecs):
        part[16:16 + vecs, v:v + 1] = jnp.sum(sums[v], axis=1, keepdims=True)
    for d in range(1, cols):
        col_sum_copy(d).start()
    col_slots[c] = part[...]
    for d in range(1, cols):
        col_sum_copy(d).wait_recv()
    half[...] = jnp.sum(col_slots[...], axis=0)
    for d in range(1, n):
        row_sum_copy(d).start()
    row_slots[r] = half[...]
    for d in range(1, n):
        row_sum_copy(d).wait_recv()
    sum_ref[...] = jnp.sum(row_slots[...], axis=0) * (1.0 / (length * n * cols))

    for d in range(1, n):
        row_copy(d).wait_send()
        row_sum_copy(d).wait_send()
    for d in range(1, cols):
        col_sum_copy(d).wait_send()


def reduce_pieces(came, tr, x_vec, residue, p_vec, gram, cols):
    n, depth, width = came.shape
    vmem = pl.BlockSpec(memory_space=pltpu.VMEM)
    dma = pltpu.SemaphoreType.DMA
    return pl.pallas_call(
        reduce_kernel,
        out_shape=(jax.ShapeDtypeStruct(x_vec.shape, F32), jax.ShapeDtypeStruct(SMALL, F32)),
        in_specs=[vmem] * 6,
        out_specs=(vmem,) * 2,
        scratch_shapes=[
            pltpu.VMEM((n - 1, depth, width), BF16),
            pltpu.VMEM((n - 1, depth, width), BF16),
            pltpu.VMEM(SMALL, F32),
            pltpu.VMEM(SMALL, F32),
            pltpu.VMEM((cols,) + SMALL, F32),
            pltpu.VMEM((n,) + SMALL, F32),
            dma((n - 1,)), dma((n - 1,)),
            dma((cols,)), dma((cols,)), dma((n,)), dma((n,)),
        ],
        compiler_params=pltpu.CompilerParams(
            collective_id=1, has_side_effects=True, vmem_limit_bytes=VMEM_BYTES),
    )(came, tr, x_vec, residue, p_vec, gram)


def body(x_vec, hx_vec, p_vec, hp_vec, theta, precond, tile_vals, tile_rows, tile_cols, tile_count):
    vecs = x_vec.shape[0]
    n = lax.axis_size("row")
    cols = lax.axis_size("col")
    places = [(r, c) for r in range(n) for c in range(cols)]
    down = [(r * cols + (c + r) % cols, r * cols + c) for r, c in places]
    up = [(target, source) for source, target in down]
    rows, columns, count = tile_rows[0, 0], tile_cols[0, 0], tile_count[0]
    own, residue, gram = gather_pieces(x_vec, hx_vec, p_vec, hp_vec, theta, precond, n)
    far = lax.ppermute(own, ("row", "col"), down)
    packed, fwd = forward_products(tile_vals[0, 0], rows, columns, count, own)
    came = lax.ppermute(fwd, ("row", "col"), up)
    tr = transposed_products(packed, rows, columns, count, far)
    hw_vec, gram = reduce_pieces(came, tr, x_vec, residue, p_vec, gram, cols)
    basis = 3 * vecs
    gram_a = jnp.concatenate(
        [gram[:basis, basis:basis + vecs], gram[16:16 + vecs, :basis].T, gram[:basis, basis + vecs:basis + 2 * vecs]], 1)
    return hw_vec, gram_a, gram[:basis, :basis]


def solution(mesh):
    placed = (
        P(None, ("col", "row")),
        P(None, ("col", "row")),
        P(None, ("col", "row")),
        P(None, ("col", "row")),
        P(),
        P(("col", "row")),
        P("row", "col", None, None),
        P("row", "col", None),
        P("row", "col", None),
        P("row", "col"),
    )
    return jax.shard_map(
        body,
        mesh=mesh,
        in_specs=placed,
        out_specs=(P(None, ("col", "row")), P(), P()),
        check_vma=False,
    )
```

```python
import functools
import jax
import jax.numpy as jnp
from jax import lax
from jax.experimental import pallas as pl
from jax.experimental.pallas import tpu as pltpu
from jax.sharding import PartitionSpec as P

BLOCK = 64
GROUPS = 4
CHUNK = 128
TOGETHER = 32
PART = 128
SMALL = (24, 128)
MESH = pl.DeviceIdType.MESH
F32 = jnp.float32
BF16 = jnp.bfloat16
VMEM_BYTES = 58 * 1024 * 1024


def row_iota():
    return lax.broadcasted_iota(jnp.int32, (8, 128), 0)


def lane_iota():
    return lax.broadcasted_iota(jnp.int32, (8, 128), 1)


def spread_matrix():
    a = lax.broadcasted_iota(jnp.int32, (128, 128), 0)
    b = lax.broadcasted_iota(jnp.int32, (128, 128), 1)
    return jnp.where((a % 64) == 2 * (b % 32) + a // 64, 1.0, 0.0).astype(BF16)


def gather_kernel(x_ref, hx_ref, theta_ref, precond_ref, own_ref, res_ref,
                  up_send, up_recv, down_send, down_recv):
    n, _, width = own_ref.shape
    vecs = x_ref.shape[0]
    r, c = lax.axis_index("row"), lax.axis_index("col")
    barrier = pltpu.get_barrier_semaphore()

    def greet(row):
        pl.semaphore_signal(barrier, inc=1, device_id=(row, c), device_id_type=MESH)

    pl.when(r > 0)(lambda: greet(r - 1))
    pl.when(r < n - 1)(lambda: greet(r + 1))
    which = lax.broadcasted_iota(jnp.int32, (vecs, 1), 0)
    theta = jnp.zeros((vecs, 1), F32)
    for k in range(vecs):
        theta = jnp.where(which == k, theta_ref[k], theta)
    for g in range(GROUPS):
        at = slice(g * width, (g + 1) * width)
        res_ref[:, at] = (hx_ref[:, at] - x_ref[:, at] * theta) / precond_ref[:, at]
    own_ref[r] = jnp.concatenate(
        [res_ref[:, g * width:(g + 1) * width] for g in range(GROUPS)], 0).astype(BF16)
    pl.semaphore_wait(barrier, jnp.where((r > 0) & (r < n - 1), 2, 1))

    def up_copy(piece, d):
        return pltpu.make_async_remote_copy(
            src_ref=own_ref.at[piece], dst_ref=own_ref.at[piece],
            send_sem=up_send.at[d], recv_sem=up_recv.at[d],
            device_id=(r + 1, c), device_id_type=MESH)

    def down_copy(piece, d):
        return pltpu.make_async_remote_copy(
            src_ref=own_ref.at[piece], dst_ref=own_ref.at[piece],
            send_sem=down_send.at[d], recv_sem=down_recv.at[d],
            device_id=(r - 1, c), device_id_type=MESH)

    pl.when(r < n - 1)(lambda: up_copy(r, 0).start())
    pl.when(r > 0)(lambda: down_copy(r, 0).start())
    for d in range(1, n):
        @pl.when(r >= d)
        def _():
            up_copy(r - d, d - 1).wait_recv()
            pl.when(r < n - 1)(lambda: up_copy(r - d, d).start())

        @pl.when(r + d < n)
        def _():
            down_copy(r + d, d - 1).wait_recv()
            pl.when(r > 0)(lambda: down_copy(r + d, d).start())

    for d in range(n):
        pl.when((r >= d) & (r < n - 1))(lambda: up_copy(r - d, d).wait_send())
        pl.when((r + d < n) & (r > 0))(lambda: down_copy(r + d, d).wait_send())


def gather_pieces(x_vec, hx_vec, theta, precond, n):
    vecs, length = x_vec.shape
    vmem = pl.BlockSpec(memory_space=pltpu.VMEM)
    dma = pltpu.SemaphoreType.DMA
    return pl.pallas_call(
        gather_kernel,
        out_shape=(
            jax.ShapeDtypeStruct((n, GROUPS * vecs, length // GROUPS), BF16),
            jax.ShapeDtypeStruct(x_vec.shape, F32),
        ),
        in_specs=[vmem] * 2 + [pl.BlockSpec(memory_space=pltpu.SMEM), vmem],
        out_specs=(vmem,) * 2,
        scratch_shapes=[dma((n,)), dma((n,)), dma((n,)), dma((n,))],
        compiler_params=pltpu.CompilerParams(
            collective_id=0, has_side_effects=True, vmem_limit_bytes=VMEM_BYTES),
    )(x_vec, hx_vec, theta, precond.reshape(1, length))


def block_at(shape, q, g, t, parity):
    per_group = 2 * (shape[2] // 128)
    return q * (GROUPS * per_group) + g * per_group + 2 * t + parity


def each_tile(shape, visit):
    n, tiles = shape[0], shape[2] // 128
    batch = min(tiles, 32)

    def some(i, _):
        q, t0 = i // (tiles // batch), (i % (tiles // batch)) * batch
        for t in range(batch):
            visit(q, t0 + t)
        return 0
    lax.fori_loop(0, n * tiles // batch, some, 0)


def expand(src_ref, dst_ref):
    low = row_iota() < 4
    keep = low == (lane_iota() < 64)
    shape = src_ref.shape

    def tile(q, t):
        s = src_ref[q, :, pl.ds(pl.multiple_of(t * 128, 128), 128)].astype(F32)
        for h in range(2):
            v = s[8 * h:8 * h + 8]
            vl = pltpu.roll(v, 64, 1)
            vs = pltpu.roll(v, 4, 0)
            vls = pltpu.roll(vl, 4, 0)
            g = 2 * h
            dst_ref[block_at(shape, q, g, t, 0)] = jnp.where(keep, jnp.where(low, v, vls), 0.0)
            dst_ref[block_at(shape, q, g, t, 1)] = jnp.where(keep, jnp.where(low, vl, vs), 0.0)
            dst_ref[block_at(shape, q, g + 1, t, 0)] = jnp.where(keep, jnp.where(low, vs, vl), 0.0)
            dst_ref[block_at(shape, q, g + 1, t, 1)] = jnp.where(keep, jnp.where(low, vls, v), 0.0)
    each_tile(shape, tile)


def fold(src_ref, dst_ref):
    low = row_iota() < 4
    keep = low == (lane_iota() < 64)
    shape = dst_ref.shape

    def tile(q, t):
        out = []
        for h in range(2):
            e0, o0, e1, o1 = [src_ref[block_at(shape, q, 2 * h + i // 2, t, i % 2)] for i in range(4)]
            stay = jnp.where(keep, jnp.where(low, e0, o1), pltpu.roll(jnp.where(low, o0, e1), 64, 1))
            move = jnp.where(keep, jnp.where(low, e1, o0), pltpu.roll(jnp.where(low, o1, e0), 64, 1))
            out.append(stay + pltpu.roll(move, 4, 0))
        at = pl.ds(pl.multiple_of(t * 128, 128), 128)
        dst_ref[q, :, at] = jnp.concatenate(out, 0).astype(dst_ref.dtype)
    each_tile(shape, tile)


def each_part(blocks, visit):
    def part(i, _):
        visit(pl.ds(i * PART, PART))
        return 0
    lax.fori_loop(0, blocks // PART, part, 0)


def forward_kernel(rows_ref, cols_ref, count_ref, vals_ref, own_ref, packed, fwd_ref, x_col, acc, loose):
    step, steps = pl.program_id(0), pl.num_programs(0)
    nblk = x_col.shape[0]
    quarter = lane_iota() // 32

    @pl.when(step == 0)
    def _():
        expand(own_ref, x_col)

        def clear(at):
            acc[at] = jnp.zeros((PART, 8, 128), F32)
        each_part(nblk, clear)

    count = count_ref[0]
    first = step * CHUNK
    live = jnp.clip(count - first, 0, CHUNK)

    def some_slots(i, _):
        base = i * TOGETHER
        for half in range(TOGETHER // 16):
            z0 = pl.multiple_of(base + half * 16, 16)
            for s in range(32):
                v = vals_ref[pl.ds(z0, 16), s * 128:(s + 1) * 128]
                loose[half, pl.ds(s, 16, stride=32), :] = v.astype(F32)
        for part in range(TOGETHER // 4):
            at = base + part * 4
            w = loose[part // 4, (part % 4) * 128:(part % 4 + 1) * 128, :].astype(BF16)
            packed[pl.ds(pl.multiple_of(at * 32, 128), 128), :] = w
            rows, lf = [], []
            for z in range(4):
                slot = first + at + z
                lf.append(x_col[cols_ref[slot]])
                rows.append(jnp.where(slot < count, rows_ref[slot], nblk))
            of = lax.dot_general(jnp.concatenate(lf, 0).astype(BF16), w, (((1,), (1,)), ((), ())),
                                 preferred_element_type=F32)
            for z in range(4):
                acc[rows[z]] += jnp.where(quarter == z, of[8 * z:8 * z + 8], 0.0)
        return 0
    lax.fori_loop(0, (live + TOGETHER - 1) // TOGETHER, some_slots, 0)

    @pl.when(step == steps - 1)
    def _():
        spread = spread_matrix()

        def part(at):
            x = acc[at].reshape(PART * 8, 128)
            hi = x.astype(BF16)
            lo = (x - hi.astype(F32)).astype(BF16)
            back = (((1,), (1,)), ((), ()))
            y = lax.dot_general(hi, spread, back, preferred_element_type=F32)
            y += lax.dot_general(lo, spread, back, preferred_element_type=F32)
            acc[at] = y.reshape(PART, 8, 128)
        each_part(nblk, part)
        fold(acc, fwd_ref)


def transposed_kernel(rows_ref, cols_ref, count_ref, packed, far_ref, tr_ref, x_row, acc):
    step, steps = pl.program_id(0), pl.num_programs(0)
    nblk = x_row.shape[0]
    quarter = lane_iota() // 32

    @pl.when(step == 0)
    def _():
        expand(far_ref, x_row)
        spread = spread_matrix()

        def part(at):
            x = x_row[at].reshape(PART * 8, 128).astype(BF16)
            x_row[at] = jnp.dot(x, spread, preferred_element_type=F32).reshape(PART, 8, 128)
            acc[at] = jnp.zeros((PART, 8, 128), F32)
        each_part(nblk, part)

    count = count_ref[0]
    first = step * CHUNK
    live = jnp.clip(count - first, 0, CHUNK)

    def some_slots(i, _):
        for part in range(TOGETHER // 4):
            at = i * TOGETHER + part * 4
            w = packed[pl.ds(pl.multiple_of(at * 32, 128), 128), :]
            cols, lt = [], []
            for z in range(4):
                slot = first + at + z
                lt.append(jnp.where(quarter == z, x_row[rows_ref[slot]], 0.0))
                cols.append(jnp.where(slot < count, cols_ref[slot], nblk))
            ot = jnp.dot(jnp.concatenate(lt, 0).astype(BF16), w, preferred_element_type=F32)
            for z in range(4):
                acc[cols[z]] += ot[8 * z:8 * z + 8]
        return 0
    lax.fori_loop(0, (live + TOGETHER - 1) // TOGETHER, some_slots, 0)

    pl.when(step == steps - 1)(lambda: fold(acc, tr_ref))


def cost(slots):
    return pl.CostEstimate(flops=slots * 4 * 128 * 128 * 64, bytes_accessed=slots * 16384, transcendentals=0)


def forward_products(vals, rows, cols, count, own):
    slots, size = vals.shape
    n, depth, width = own.shape
    nblk = n * GROUPS * (width // 64)
    whole = pl.BlockSpec((n, depth, width), lambda i, *_: (0, 0, 0))
    tall = CHUNK * size // 128
    return pl.pallas_call(
        forward_kernel,
        out_shape=(jax.ShapeDtypeStruct((slots * size // 128, 128), BF16), jax.ShapeDtypeStruct(own.shape, BF16)),
        grid_spec=pltpu.PrefetchScalarGridSpec(
            num_scalar_prefetch=3,
            grid=(slots // CHUNK,),
            in_specs=[pl.BlockSpec((CHUNK, size), lambda i, *_: (i, 0)), whole],
            out_specs=(pl.BlockSpec((tall, 128), lambda i, *_: (i, 0)), whole),
            scratch_shapes=[
                pltpu.VMEM((nblk, 8, 128), F32),
                pltpu.VMEM((nblk + 1, 8, 128), F32),
                pltpu.VMEM((TOGETHER // 16, 512, 128), F32),
            ],
        ),
        cost_estimate=cost(slots),
        compiler_params=pltpu.CompilerParams(vmem_limit_bytes=VMEM_BYTES),
    )(rows, cols, count, vals, own)


def transposed_products(packed, rows, cols, count, far):
    slots = rows.shape[0]
    n, depth, width = far.shape
    nblk = n * GROUPS * (width // 64)
    whole = pl.BlockSpec((n, depth, width), lambda i, *_: (0, 0, 0))
    tall = CHUNK * packed.shape[0] // slots
    return pl.pallas_call(
        transposed_kernel,
        out_shape=jax.ShapeDtypeStruct(far.shape, F32),
        grid_spec=pltpu.PrefetchScalarGridSpec(
            num_scalar_prefetch=3,
            grid=(slots // CHUNK,),
            in_specs=[pl.BlockSpec((tall, 128), lambda i, *_: (i, 0)), whole],
            out_specs=whole,
            scratch_shapes=[
                pltpu.VMEM((nblk, 8, 128), F32),
                pltpu.VMEM((nblk + 1, 8, 128), F32),
            ],
        ),
        cost_estimate=cost(slots),
        compiler_params=pltpu.CompilerParams(vmem_limit_bytes=VMEM_BYTES),
    )(rows, cols, count, packed, far)


def reduce_kernel(came_ref, tr_ref, x_ref, res_ref, p_ref, hx_ref, hp_ref, out_ref, sum_ref,
                  stage, landed, part, half, col_slots, row_slots,
                  send, recv, col_send, col_recv, row_send, row_recv):
    n, _, width = came_ref.shape
    vecs, length = x_ref.shape
    cols = lax.axis_size("col")
    r, c = lax.axis_index("row"), lax.axis_index("col")
    barrier = pltpu.get_barrier_semaphore()
    for d in range(1, n):
        pl.semaphore_signal(barrier, inc=1, device_id=(lax.rem(r + d, n), c), device_id_type=MESH)
    for d in range(1, cols):
        pl.semaphore_signal(barrier, inc=1, device_id=(r, lax.rem(c + d, cols)), device_id_type=MESH)

    def row_copy(d):
        return pltpu.make_async_remote_copy(
            src_ref=stage.at[d - 1], dst_ref=landed.at[d - 1],
            send_sem=send.at[d - 1], recv_sem=recv.at[d - 1],
            device_id=(lax.rem(r + d, n), c), device_id_type=MESH)

    def col_sum_copy(d):
        return pltpu.make_async_remote_copy(
            src_ref=part, dst_ref=col_slots.at[c],
            send_sem=col_send.at[d], recv_sem=col_recv.at[d],
            device_id=(r, lax.rem(c + d, cols)), device_id_type=MESH)

    def row_sum_copy(d):
        return pltpu.make_async_remote_copy(
            src_ref=half, dst_ref=row_slots.at[r],
            send_sem=row_send.at[d], recv_sem=row_recv.at[d],
            device_id=(lax.rem(r + d, n), c), device_id_type=MESH)

    def summed(d):
        q = lax.rem(r + d, n)
        return tr_ref[q] + came_ref[q].astype(F32)

    for d in range(1, n):
        stage[d - 1] = summed(d).astype(BF16)
        if d == 1:
            pl.semaphore_wait(barrier, n + cols - 2)
        row_copy(d).start()
    span = min(length, 2048)
    left = [x_ref, res_ref, p_ref]
    right = left + [hx_ref, hp_ref]

    def early(i, gram):
        at = pl.ds(pl.multiple_of(i * span, span), span)
        v = jnp.concatenate([ref[:, at] for ref in left], 0)
        w = jnp.concatenate([ref[:, at] for ref in right], 0)
        return gram + lax.dot_general(v, w, (((1,), (1,)), ((), ())), precision=lax.Precision.HIGHEST,
                                      preferred_element_type=F32)

    part[...] = jnp.zeros_like(part)
    part[:3 * vecs, :5 * vecs] = lax.fori_loop(0, length // span, early, jnp.zeros((3 * vecs, 5 * vecs), F32))
    total = summed(0)
    for d in range(1, n):
        row_copy(d).wait_recv()
        total += landed[d - 1].astype(F32)
    for g in range(GROUPS):
        out_ref[:, g * width:(g + 1) * width] = total[4 * g:4 * g + 4]

    def dots(i, sums):
        sums = list(sums)
        for t in range(8):
            at = pl.ds(pl.multiple_of((i * 8 + t) * 128, 128), 128)
            hw = out_ref[:, at]
            for v in range(3 * vecs):
                row = (x_ref, res_ref, p_ref)[v // vecs][v % vecs:v % vecs + 1, at]
                sums[v] = sums[v] + row * hw
        return tuple(sums)

    sums = lax.fori_loop(0, length // 1024, dots, tuple(jnp.zeros((vecs, 128), F32) for _ in range(3 * vecs)))
    for v in range(3 * vecs):
        part[16:16 + vecs, v:v + 1] = jnp.sum(sums[v], axis=1, keepdims=True)
    for d in range(1, cols):
        col_sum_copy(d).start()
    col_slots[c] = part[...]
    for d in range(1, cols):
        col_sum_copy(d).wait_recv()
    half[...] = jnp.sum(col_slots[...], axis=0)
    for d in range(1, n):
        row_sum_copy(d).start()
    row_slots[r] = half[...]
    for d in range(1, n):
        row_sum_copy(d).wait_recv()
    sum_ref[...] = jnp.sum(row_slots[...], axis=0) * (1.0 / (length * n * cols))

    for d in range(1, n):
        row_copy(d).wait_send()
        row_sum_copy(d).wait_send()
    for d in range(1, cols):
        col_sum_copy(d).wait_send()


def reduce_pieces(came, tr, x_vec, residue, p_vec, hx_vec, hp_vec, cols):
    n, depth, width = came.shape
    vmem = pl.BlockSpec(memory_space=pltpu.VMEM)
    dma = pltpu.SemaphoreType.DMA
    return pl.pallas_call(
        reduce_kernel,
        out_shape=(jax.ShapeDtypeStruct(x_vec.shape, F32), jax.ShapeDtypeStruct(SMALL, F32)),
        in_specs=[vmem] * 7,
        out_specs=(vmem,) * 2,
        scratch_shapes=[
            pltpu.VMEM((n - 1, depth, width), BF16),
            pltpu.VMEM((n - 1, depth, width), BF16),
            pltpu.VMEM(SMALL, F32),
            pltpu.VMEM(SMALL, F32),
            pltpu.VMEM((cols,) + SMALL, F32),
            pltpu.VMEM((n,) + SMALL, F32),
            dma((n - 1,)), dma((n - 1,)),
            dma((cols,)), dma((cols,)), dma((n,)), dma((n,)),
        ],
        compiler_params=pltpu.CompilerParams(
            collective_id=1, has_side_effects=True, vmem_limit_bytes=VMEM_BYTES),
    )(came, tr, x_vec, residue, p_vec, hx_vec, hp_vec)


def finish_kernel(hw_ref, sum_ref, out_ref, a_ref, b_ref):
    out_ref[...] = hw_ref[...]
    vecs = hw_ref.shape[0]
    basis = 3 * vecs
    gram = sum_ref[...]
    b_ref[...] = gram[:basis, :basis]
    a_ref[:, :vecs] = gram[:basis, basis:basis + vecs]
    turned = jnp.transpose(gram[16:24])
    a_ref[:, vecs:2 * vecs] = turned[:basis, :vecs]
    a_ref[:, 2 * vecs:] = gram[:basis, basis + vecs:basis + 2 * vecs]


def finish(hw_vec, gram):
    basis = 3 * hw_vec.shape[0]
    vmem = pl.BlockSpec(memory_space=pltpu.VMEM)
    square = jax.ShapeDtypeStruct((basis, basis), F32)
    return pl.pallas_call(
        finish_kernel,
        out_shape=(jax.ShapeDtypeStruct(hw_vec.shape, F32), square, square),
        in_specs=[vmem] * 2,
        out_specs=(vmem,) * 3,
    )(hw_vec, gram)


def body(x_vec, hx_vec, p_vec, hp_vec, theta, precond, tile_vals, tile_rows, tile_cols, tile_count):
    n = lax.axis_size("row")
    cols = lax.axis_size("col")
    places = [(r, c) for r in range(n) for c in range(cols)]
    down = [(r * cols + (c + r) % cols, r * cols + c) for r, c in places]
    up = [(target, source) for source, target in down]
    rows, columns, count = tile_rows[0, 0], tile_cols[0, 0], tile_count[0]
    own, residue = gather_pieces(x_vec, hx_vec, theta, precond, n)
    far = lax.ppermute(own, ("row", "col"), down)
    packed, fwd = forward_products(tile_vals[0, 0], rows, columns, count, own)
    came = lax.ppermute(fwd, ("row", "col"), up)
    tr = transposed_products(packed, rows, columns, count, far)
    hw_vec, gram = reduce_pieces(came, tr, x_vec, residue, p_vec, hx_vec, hp_vec, cols)
    return finish(hw_vec, gram)


def solution(mesh):
    placed = (
        P(None, ("col", "row")),
        P(None, ("col", "row")),
        P(None, ("col", "row")),
        P(None, ("col", "row")),
        P(),
        P(("col", "row")),
        P("row", "col", None, None),
        P("row", "col", None),
        P("row", "col", None),
        P("row", "col"),
    )
    return jax.shard_map(
        body,
        mesh=mesh,
        in_specs=placed,
        out_specs=(P(None, ("col", "row")), P(), P()),
        check_vma=False,
    )
```

```python
import functools
import jax
import jax.numpy as jnp
from jax import lax
from jax.experimental import pallas as pl
from jax.experimental.pallas import tpu as pltpu
from jax.sharding import PartitionSpec as P

BLOCK = 64
GROUPS = 4
CHUNK = 256
TOGETHER = 32
PART = 128
SMALL = (24, 128)
MESH = pl.DeviceIdType.MESH
F32 = jnp.float32
BF16 = jnp.bfloat16
VMEM_BYTES = 32 * 1024 * 1024


def row_iota():
    return lax.broadcasted_iota(jnp.int32, (8, 128), 0)


def lane_iota():
    return lax.broadcasted_iota(jnp.int32, (8, 128), 1)


def spread_matrix():
    a = lax.broadcasted_iota(jnp.int32, (128, 128), 0)
    b = lax.broadcasted_iota(jnp.int32, (128, 128), 1)
    return jnp.where((a % 64) == 2 * (b % 32) + a // 64, 1.0, 0.0).astype(BF16)


def gather_kernel(x_ref, hx_ref, theta_ref, precond_ref, own_ref, res_ref,
                  up_send, up_recv, down_send, down_recv):
    n, _, width = own_ref.shape
    vecs = x_ref.shape[0]
    r, c = lax.axis_index("row"), lax.axis_index("col")
    barrier = pltpu.get_barrier_semaphore()

    def greet(row):
        pl.semaphore_signal(barrier, inc=1, device_id=(row, c), device_id_type=MESH)

    pl.when(r > 0)(lambda: greet(r - 1))
    pl.when(r < n - 1)(lambda: greet(r + 1))
    which = lax.broadcasted_iota(jnp.int32, (vecs, 1), 0)
    theta = jnp.zeros((vecs, 1), F32)
    for k in range(vecs):
        theta = jnp.where(which == k, theta_ref[k], theta)
    for g in range(GROUPS):
        at = slice(g * width, (g + 1) * width)
        res_ref[:, at] = (hx_ref[:, at] - x_ref[:, at] * theta) / precond_ref[:, at]
    own_ref[r] = jnp.concatenate(
        [res_ref[:, g * width:(g + 1) * width] for g in range(GROUPS)], 0).astype(BF16)
    pl.semaphore_wait(barrier, jnp.where((r > 0) & (r < n - 1), 2, 1))

    def up_copy(piece, d):
        return pltpu.make_async_remote_copy(
            src_ref=own_ref.at[piece], dst_ref=own_ref.at[piece],
            send_sem=up_send.at[d], recv_sem=up_recv.at[d],
            device_id=(r + 1, c), device_id_type=MESH)

    def down_copy(piece, d):
        return pltpu.make_async_remote_copy(
            src_ref=own_ref.at[piece], dst_ref=own_ref.at[piece],
            send_sem=down_send.at[d], recv_sem=down_recv.at[d],
            device_id=(r - 1, c), device_id_type=MESH)

    pl.when(r < n - 1)(lambda: up_copy(r, 0).start())
    pl.when(r > 0)(lambda: down_copy(r, 0).start())
    for d in range(1, n):
        @pl.when(r >= d)
        def _():
            up_copy(r - d, d - 1).wait_recv()
            pl.when(r < n - 1)(lambda: up_copy(r - d, d).start())

        @pl.when(r + d < n)
        def _():
            down_copy(r + d, d - 1).wait_recv()
            pl.when(r > 0)(lambda: down_copy(r + d, d).start())

    for d in range(n):
        pl.when((r >= d) & (r < n - 1))(lambda: up_copy(r - d, d).wait_send())
        pl.when((r + d < n) & (r > 0))(lambda: down_copy(r + d, d).wait_send())


def gather_pieces(x_vec, hx_vec, theta, precond, n):
    vecs, length = x_vec.shape
    vmem = pl.BlockSpec(memory_space=pltpu.VMEM)
    dma = pltpu.SemaphoreType.DMA
    return pl.pallas_call(
        gather_kernel,
        out_shape=(
            jax.ShapeDtypeStruct((n, GROUPS * vecs, length // GROUPS), BF16),
            jax.ShapeDtypeStruct(x_vec.shape, F32),
        ),
        in_specs=[vmem] * 2 + [pl.BlockSpec(memory_space=pltpu.SMEM), vmem],
        out_specs=(vmem,) * 2,
        scratch_shapes=[dma((n,)), dma((n,)), dma((n,)), dma((n,))],
        compiler_params=pltpu.CompilerParams(
            collective_id=0, has_side_effects=True, vmem_limit_bytes=VMEM_BYTES),
    )(x_vec, hx_vec, theta, precond.reshape(1, length))


def block_at(shape, q, g, t, parity):
    per_group = 2 * (shape[2] // 128)
    return q * (GROUPS * per_group) + g * per_group + 2 * t + parity


def each_tile(shape, visit):
    n, tiles = shape[0], shape[2] // 128
    batch = min(tiles, 32)

    def some(i, _):
        q, t0 = i // (tiles // batch), (i % (tiles // batch)) * batch
        for t in range(batch):
            visit(q, t0 + t)
        return 0
    lax.fori_loop(0, n * tiles // batch, some, 0)


def expand(src_ref, dst_ref):
    low = row_iota() < 4
    keep = low == (lane_iota() < 64)
    shape = src_ref.shape

    def tile(q, t):
        s = src_ref[q, :, pl.ds(pl.multiple_of(t * 128, 128), 128)].astype(F32)
        for h in range(2):
            v = s[8 * h:8 * h + 8]
            vl = pltpu.roll(v, 64, 1)
            vs = pltpu.roll(v, 4, 0)
            vls = pltpu.roll(vl, 4, 0)
            g = 2 * h
            dst_ref[block_at(shape, q, g, t, 0)] = jnp.where(keep, jnp.where(low, v, vls), 0.0)
            dst_ref[block_at(shape, q, g, t, 1)] = jnp.where(keep, jnp.where(low, vl, vs), 0.0)
            dst_ref[block_at(shape, q, g + 1, t, 0)] = jnp.where(keep, jnp.where(low, vs, vl), 0.0)
            dst_ref[block_at(shape, q, g + 1, t, 1)] = jnp.where(keep, jnp.where(low, vls, v), 0.0)
    each_tile(shape, tile)


def fold(src_ref, dst_ref):
    low = row_iota() < 4
    keep = low == (lane_iota() < 64)
    shape = dst_ref.shape

    def tile(q, t):
        out = []
        for h in range(2):
            e0, o0, e1, o1 = [src_ref[block_at(shape, q, 2 * h + i // 2, t, i % 2)] for i in range(4)]
            stay = jnp.where(keep, jnp.where(low, e0, o1), pltpu.roll(jnp.where(low, o0, e1), 64, 1))
            move = jnp.where(keep, jnp.where(low, e1, o0), pltpu.roll(jnp.where(low, o1, e0), 64, 1))
            out.append(stay + pltpu.roll(move, 4, 0))
        at = pl.ds(pl.multiple_of(t * 128, 128), 128)
        dst_ref[q, :, at] = jnp.concatenate(out, 0).astype(dst_ref.dtype)
    each_tile(shape, tile)


def each_part(blocks, visit):
    def part(i, _):
        visit(pl.ds(i * PART, PART))
        return 0
    lax.fori_loop(0, blocks // PART, part, 0)


def forward_kernel(rows_ref, cols_ref, count_ref, vals_ref, own_ref, packed, fwd_ref, x_col, acc, loose):
    step, steps = pl.program_id(0), pl.num_programs(0)
    nblk = x_col.shape[0]
    quarter = lane_iota() // 32

    @pl.when(step == 0)
    def _():
        expand(own_ref, x_col)

        def clear(at):
            acc[at] = jnp.zeros((PART, 8, 128), F32)
        each_part(nblk, clear)

    count = count_ref[0]
    first = step * CHUNK
    live = jnp.clip(count - first, 0, CHUNK)

    def some_slots(i, _):
        base = i * TOGETHER
        for half in range(TOGETHER // 16):
            z0 = pl.multiple_of(base + half * 16, 16)
            for s in range(32):
                v = vals_ref[pl.ds(z0, 16), s * 128:(s + 1) * 128]
                loose[half, pl.ds(s, 16, stride=32), :] = v.astype(F32)
        for part in range(TOGETHER // 4):
            at = base + part * 4
            w = loose[part // 4, (part % 4) * 128:(part % 4 + 1) * 128, :].astype(BF16)
            packed[pl.ds(pl.multiple_of(at * 32, 128), 128), :] = w
            rows, lf = [], []
            for z in range(4):
                slot = first + at + z
                lf.append(x_col[cols_ref[slot]])
                rows.append(jnp.where(slot < count, rows_ref[slot], nblk))
            of = lax.dot_general(jnp.concatenate(lf, 0).astype(BF16), w, (((1,), (1,)), ((), ())),
                                 preferred_element_type=F32)
            for z in range(4):
                acc[rows[z]] += jnp.where(quarter == z, of[8 * z:8 * z + 8], 0.0)
        return 0
    lax.fori_loop(0, (live + TOGETHER - 1) // TOGETHER, some_slots, 0)

    @pl.when(step == steps - 1)
    def _():
        spread = spread_matrix()

        def part(at):
            x = acc[at].reshape(PART * 8, 128)
            hi = x.astype(BF16)
            lo = (x - hi.astype(F32)).astype(BF16)
            back = (((1,), (1,)), ((), ()))
            y = lax.dot_general(hi, spread, back, preferred_element_type=F32)
            y += lax.dot_general(lo, spread, back, preferred_element_type=F32)
            acc[at] = y.reshape(PART, 8, 128)
        each_part(nblk, part)
        fold(acc, fwd_ref)


def transposed_kernel(rows_ref, cols_ref, count_ref, packed, far_ref, tr_ref, x_row, acc):
    step, steps = pl.program_id(0), pl.num_programs(0)
    nblk = x_row.shape[0]
    quarter = lane_iota() // 32

    @pl.when(step == 0)
    def _():
        expand(far_ref, x_row)
        spread = spread_matrix()

        def part(at):
            x = x_row[at].reshape(PART * 8, 128).astype(BF16)
            x_row[at] = jnp.dot(x, spread, preferred_element_type=F32).reshape(PART, 8, 128)
            acc[at] = jnp.zeros((PART, 8, 128), F32)
        each_part(nblk, part)

    count = count_ref[0]
    first = step * CHUNK
    live = jnp.clip(count - first, 0, CHUNK)

    def some_slots(i, _):
        for part in range(TOGETHER // 4):
            at = i * TOGETHER + part * 4
            w = packed[pl.ds(pl.multiple_of(at * 32, 128), 128), :]
            cols, lt = [], []
            for z in range(4):
                slot = first + at + z
                lt.append(jnp.where(quarter == z, x_row[rows_ref[slot]], 0.0))
                cols.append(jnp.where(slot < count, cols_ref[slot], nblk))
            ot = jnp.dot(jnp.concatenate(lt, 0).astype(BF16), w, preferred_element_type=F32)
            for z in range(4):
                acc[cols[z]] += ot[8 * z:8 * z + 8]
        return 0
    lax.fori_loop(0, (live + TOGETHER - 1) // TOGETHER, some_slots, 0)

    pl.when(step == steps - 1)(lambda: fold(acc, tr_ref))


def cost(slots):
    return pl.CostEstimate(flops=slots * 4 * 128 * 128 * 64, bytes_accessed=slots * 16384, transcendentals=0)


def forward_products(vals, rows, cols, count, own):
    slots, size = vals.shape
    n, depth, width = own.shape
    nblk = n * GROUPS * (width // 64)
    whole = pl.BlockSpec((n, depth, width), lambda i, *_: (0, 0, 0))
    tall = CHUNK * size // 128
    return pl.pallas_call(
        forward_kernel,
        out_shape=(jax.ShapeDtypeStruct((slots * size // 128, 128), BF16), jax.ShapeDtypeStruct(own.shape, BF16)),
        grid_spec=pltpu.PrefetchScalarGridSpec(
            num_scalar_prefetch=3,
            grid=(slots // CHUNK,),
            in_specs=[pl.BlockSpec((CHUNK, size), lambda i, *_: (i, 0)), whole],
            out_specs=(pl.BlockSpec((tall, 128), lambda i, *_: (i, 0)), whole),
            scratch_shapes=[
                pltpu.VMEM((nblk, 8, 128), F32),
                pltpu.VMEM((nblk + 1, 8, 128), F32),
                pltpu.VMEM((TOGETHER // 16, 512, 128), F32),
            ],
        ),
        cost_estimate=cost(slots),
        compiler_params=pltpu.CompilerParams(vmem_limit_bytes=VMEM_BYTES),
    )(rows, cols, count, vals, own)


def transposed_products(packed, rows, cols, count, far):
    slots = rows.shape[0]
    n, depth, width = far.shape
    nblk = n * GROUPS * (width // 64)
    whole = pl.BlockSpec((n, depth, width), lambda i, *_: (0, 0, 0))
    tall = CHUNK * packed.shape[0] // slots
    return pl.pallas_call(
        transposed_kernel,
        out_shape=jax.ShapeDtypeStruct(far.shape, F32),
        grid_spec=pltpu.PrefetchScalarGridSpec(
            num_scalar_prefetch=3,
            grid=(slots // CHUNK,),
            in_specs=[pl.BlockSpec((tall, 128), lambda i, *_: (i, 0)), whole],
            out_specs=whole,
            scratch_shapes=[
                pltpu.VMEM((nblk, 8, 128), F32),
                pltpu.VMEM((nblk + 1, 8, 128), F32),
            ],
        ),
        cost_estimate=cost(slots),
        compiler_params=pltpu.CompilerParams(vmem_limit_bytes=VMEM_BYTES),
    )(rows, cols, count, packed, far)


def reduce_kernel(came_ref, tr_ref, x_ref, res_ref, p_ref, hx_ref, hp_ref, out_ref, sum_ref,
                  stage, landed, part, half, col_slots, row_slots,
                  send, recv, col_send, col_recv, row_send, row_recv):
    n, _, width = came_ref.shape
    vecs, length = x_ref.shape
    cols = lax.axis_size("col")
    r, c = lax.axis_index("row"), lax.axis_index("col")
    barrier = pltpu.get_barrier_semaphore()
    for d in range(1, n):
        pl.semaphore_signal(barrier, inc=1, device_id=(lax.rem(r + d, n), c), device_id_type=MESH)
    for d in range(1, cols):
        pl.semaphore_signal(barrier, inc=1, device_id=(r, lax.rem(c + d, cols)), device_id_type=MESH)

    def row_copy(d):
        return pltpu.make_async_remote_copy(
            src_ref=stage.at[d - 1], dst_ref=landed.at[d - 1],
            send_sem=send.at[d - 1], recv_sem=recv.at[d - 1],
            device_id=(lax.rem(r + d, n), c), device_id_type=MESH)

    def col_sum_copy(d):
        return pltpu.make_async_remote_copy(
            src_ref=part, dst_ref=col_slots.at[c],
            send_sem=col_send.at[d], recv_sem=col_recv.at[d],
            device_id=(r, lax.rem(c + d, cols)), device_id_type=MESH)

    def row_sum_copy(d):
        return pltpu.make_async_remote_copy(
            src_ref=half, dst_ref=row_slots.at[r],
            send_sem=row_send.at[d], recv_sem=row_recv.at[d],
            device_id=(lax.rem(r + d, n), c), device_id_type=MESH)

    def summed(d):
        q = lax.rem(r + d, n)
        return tr_ref[q] + came_ref[q].astype(F32)

    for d in range(1, n):
        stage[d - 1] = summed(d).astype(BF16)
        if d == 1:
            pl.semaphore_wait(barrier, n + cols - 2)
        row_copy(d).start()
    span = min(length, 2048)
    left = [x_ref, res_ref, p_ref]
    right = left + [hx_ref, hp_ref]

    def early(i, gram):
        at = pl.ds(pl.multiple_of(i * span, span), span)
        v = jnp.concatenate([ref[:, at] for ref in left], 0)
        w = jnp.concatenate([ref[:, at] for ref in right], 0)
        return gram + lax.dot_general(v, w, (((1,), (1,)), ((), ())), precision=lax.Precision.HIGHEST,
                                      preferred_element_type=F32)

    part[...] = jnp.zeros_like(part)
    part[:3 * vecs, :5 * vecs] = lax.fori_loop(0, length // span, early, jnp.zeros((3 * vecs, 5 * vecs), F32))
    total = summed(0)
    for d in range(1, n):
        row_copy(d).wait_recv()
        total += landed[d - 1].astype(F32)
    for g in range(GROUPS):
        out_ref[:, g * width:(g + 1) * width] = total[4 * g:4 * g + 4]

    def dots(i, sums):
        sums = list(sums)
        for t in range(8):
            at = pl.ds(pl.multiple_of((i * 8 + t) * 128, 128), 128)
            hw = out_ref[:, at]
            for v in range(3 * vecs):
                row = (x_ref, res_ref, p_ref)[v // vecs][v % vecs:v % vecs + 1, at]
                sums[v] = sums[v] + row * hw
        return tuple(sums)

    sums = lax.fori_loop(0, length // 1024, dots, tuple(jnp.zeros((vecs, 128), F32) for _ in range(3 * vecs)))
    for v in range(3 * vecs):
        part[16:16 + vecs, v:v + 1] = jnp.sum(sums[v], axis=1, keepdims=True)
    for d in range(1, cols):
        col_sum_copy(d).start()
    col_slots[c] = part[...]
    for d in range(1, cols):
        col_sum_copy(d).wait_recv()
    half[...] = jnp.sum(col_slots[...], axis=0)
    for d in range(1, n):
        row_sum_copy(d).start()
    row_slots[r] = half[...]
    for d in range(1, n):
        row_sum_copy(d).wait_recv()
    sum_ref[...] = jnp.sum(row_slots[...], axis=0) * (1.0 / (length * n * cols))

    for d in range(1, n):
        row_copy(d).wait_send()
        row_sum_copy(d).wait_send()
    for d in range(1, cols):
        col_sum_copy(d).wait_send()


def reduce_pieces(came, tr, x_vec, residue, p_vec, hx_vec, hp_vec, cols):
    n, depth, width = came.shape
    vmem = pl.BlockSpec(memory_space=pltpu.VMEM)
    dma = pltpu.SemaphoreType.DMA
    return pl.pallas_call(
        reduce_kernel,
        out_shape=(jax.ShapeDtypeStruct(x_vec.shape, F32), jax.ShapeDtypeStruct(SMALL, F32)),
        in_specs=[vmem] * 7,
        out_specs=(vmem,) * 2,
        scratch_shapes=[
            pltpu.VMEM((n - 1, depth, width), BF16),
            pltpu.VMEM((n - 1, depth, width), BF16),
            pltpu.VMEM(SMALL, F32),
            pltpu.VMEM(SMALL, F32),
            pltpu.VMEM((cols,) + SMALL, F32),
            pltpu.VMEM((n,) + SMALL, F32),
            dma((n - 1,)), dma((n - 1,)),
            dma((cols,)), dma((cols,)), dma((n,)), dma((n,)),
        ],
        compiler_params=pltpu.CompilerParams(
            collective_id=1, has_side_effects=True, vmem_limit_bytes=VMEM_BYTES),
    )(came, tr, x_vec, residue, p_vec, hx_vec, hp_vec)


def finish_kernel(hw_ref, sum_ref, out_ref, a_ref, b_ref):
    out_ref[...] = hw_ref[...]
    vecs = hw_ref.shape[0]
    basis = 3 * vecs
    gram = sum_ref[...]
    b_ref[...] = gram[:basis, :basis]
    a_ref[:, :vecs] = gram[:basis, basis:basis + vecs]
    turned = jnp.transpose(gram[16:24])
    a_ref[:, vecs:2 * vecs] = turned[:basis, :vecs]
    a_ref[:, 2 * vecs:] = gram[:basis, basis + vecs:basis + 2 * vecs]


def finish(hw_vec, gram):
    basis = 3 * hw_vec.shape[0]
    vmem = pl.BlockSpec(memory_space=pltpu.VMEM)
    square = jax.ShapeDtypeStruct((basis, basis), F32)
    return pl.pallas_call(
        finish_kernel,
        out_shape=(jax.ShapeDtypeStruct(hw_vec.shape, F32), square, square),
        in_specs=[vmem] * 2,
        out_specs=(vmem,) * 3,
    )(hw_vec, gram)


def body(x_vec, hx_vec, p_vec, hp_vec, theta, precond, tile_vals, tile_rows, tile_cols, tile_count):
    n = lax.axis_size("row")
    cols = lax.axis_size("col")
    places = [(r, c) for r in range(n) for c in range(cols)]
    down = [(r * cols + (c + r) % cols, r * cols + c) for r, c in places]
    up = [(target, source) for source, target in down]
    rows, columns, count = tile_rows[0, 0], tile_cols[0, 0], tile_count[0]
    own, residue = gather_pieces(x_vec, hx_vec, theta, precond, n)
    far = lax.ppermute(own, ("row", "col"), down)
    packed, fwd = forward_products(tile_vals[0, 0], rows, columns, count, own)
    came = lax.ppermute(fwd, ("row", "col"), up)
    tr = transposed_products(packed, rows, columns, count, far)
    hw_vec, gram = reduce_pieces(came, tr, x_vec, residue, p_vec, hx_vec, hp_vec, cols)
    return finish(hw_vec, gram)


def solution(mesh):
    placed = (
        P(None, ("col", "row")),
        P(None, ("col", "row")),
        P(None, ("col", "row")),
        P(None, ("col", "row")),
        P(),
        P(("col", "row")),
        P("row", "col", None, None),
        P("row", "col", None),
        P("row", "col", None),
        P("row", "col"),
    )
    return jax.shard_map(
        body,
        mesh=mesh,
        in_specs=placed,
        out_specs=(P(None, ("col", "row")), P(), P()),
        check_vma=False,
    )
```

```python
import functools
import jax
import jax.numpy as jnp
from jax import lax
from jax.experimental import pallas as pl
from jax.experimental.pallas import tpu as pltpu
from jax.sharding import PartitionSpec as P

BLOCK = 64
GROUPS = 4
CHUNK = 256
TOGETHER = 32
PART = 128
SMALL = (24, 128)
MESH = pl.DeviceIdType.MESH
F32 = jnp.float32
BF16 = jnp.bfloat16
VMEM_BYTES = 32 * 1024 * 1024
GATHER_VMEM_BYTES = 58 * 1024 * 1024


def row_iota():
    return lax.broadcasted_iota(jnp.int32, (8, 128), 0)


def lane_iota():
    return lax.broadcasted_iota(jnp.int32, (8, 128), 1)


def spread_matrix():
    a = lax.broadcasted_iota(jnp.int32, (128, 128), 0)
    b = lax.broadcasted_iota(jnp.int32, (128, 128), 1)
    return jnp.where((a % 64) == 2 * (b % 32) + a // 64, 1.0, 0.0).astype(BF16)


def gather_kernel(x_ref, hx_ref, theta_ref, precond_ref, own_ref, res_ref,
                  up_send, up_recv, down_send, down_recv):
    n, _, width = own_ref.shape
    vecs = x_ref.shape[0]
    r, c = lax.axis_index("row"), lax.axis_index("col")
    barrier = pltpu.get_barrier_semaphore()

    def greet(row):
        pl.semaphore_signal(barrier, inc=1, device_id=(row, c), device_id_type=MESH)

    pl.when(r > 0)(lambda: greet(r - 1))
    pl.when(r < n - 1)(lambda: greet(r + 1))
    which = lax.broadcasted_iota(jnp.int32, (vecs, 1), 0)
    theta = jnp.zeros((vecs, 1), F32)
    for k in range(vecs):
        theta = jnp.where(which == k, theta_ref[k], theta)
    for g in range(GROUPS):
        at = slice(g * width, (g + 1) * width)
        res_ref[:, at] = (hx_ref[:, at] - x_ref[:, at] * theta) / precond_ref[:, at]
    own_ref[r] = jnp.concatenate(
        [res_ref[:, g * width:(g + 1) * width] for g in range(GROUPS)], 0).astype(BF16)
    pl.semaphore_wait(barrier, jnp.where((r > 0) & (r < n - 1), 2, 1))

    def up_copy(piece, d):
        return pltpu.make_async_remote_copy(
            src_ref=own_ref.at[piece], dst_ref=own_ref.at[piece],
            send_sem=up_send.at[d], recv_sem=up_recv.at[d],
            device_id=(r + 1, c), device_id_type=MESH)

    def down_copy(piece, d):
        return pltpu.make_async_remote_copy(
            src_ref=own_ref.at[piece], dst_ref=own_ref.at[piece],
            send_sem=down_send.at[d], recv_sem=down_recv.at[d],
            device_id=(r - 1, c), device_id_type=MESH)

    pl.when(r < n - 1)(lambda: up_copy(r, 0).start())
    pl.when(r > 0)(lambda: down_copy(r, 0).start())
    for d in range(1, n):
        @pl.when(r >= d)
        def _():
            up_copy(r - d, d - 1).wait_recv()
            pl.when(r < n - 1)(lambda: up_copy(r - d, d).start())

        @pl.when(r + d < n)
        def _():
            down_copy(r + d, d - 1).wait_recv()
            pl.when(r > 0)(lambda: down_copy(r + d, d).start())

    for d in range(n):
        pl.when((r >= d) & (r < n - 1))(lambda: up_copy(r - d, d).wait_send())
        pl.when((r + d < n) & (r > 0))(lambda: down_copy(r + d, d).wait_send())


def gather_pieces(x_vec, hx_vec, theta, precond, n):
    vecs, length = x_vec.shape
    vmem = pl.BlockSpec(memory_space=pltpu.VMEM)
    dma = pltpu.SemaphoreType.DMA
    return pl.pallas_call(
        gather_kernel,
        out_shape=(
            jax.ShapeDtypeStruct((n, GROUPS * vecs, length // GROUPS), BF16),
            jax.ShapeDtypeStruct(x_vec.shape, F32),
        ),
        in_specs=[vmem] * 2 + [pl.BlockSpec(memory_space=pltpu.SMEM), vmem],
        out_specs=(vmem,) * 2,
        scratch_shapes=[dma((n,)), dma((n,)), dma((n,)), dma((n,))],
        compiler_params=pltpu.CompilerParams(
            collective_id=0, has_side_effects=True, vmem_limit_bytes=GATHER_VMEM_BYTES),
    )(x_vec, hx_vec, theta, precond.reshape(1, length))


def block_at(shape, q, g, t, parity):
    per_group = 2 * (shape[2] // 128)
    return q * (GROUPS * per_group) + g * per_group + 2 * t + parity


def each_tile(shape, visit):
    n, tiles = shape[0], shape[2] // 128
    batch = min(tiles, 32)

    def some(i, _):
        q, t0 = i // (tiles // batch), (i % (tiles // batch)) * batch
        for t in range(batch):
            visit(q, t0 + t)
        return 0
    lax.fori_loop(0, n * tiles // batch, some, 0)


def expand(src_ref, dst_ref):
    low = row_iota() < 4
    keep = low == (lane_iota() < 64)
    shape = src_ref.shape

    def tile(q, t):
        s = src_ref[q, :, pl.ds(pl.multiple_of(t * 128, 128), 128)].astype(F32)
        for h in range(2):
            v = s[8 * h:8 * h + 8]
            vl = pltpu.roll(v, 64, 1)
            vs = pltpu.roll(v, 4, 0)
            vls = pltpu.roll(vl, 4, 0)
            g = 2 * h
            dst_ref[block_at(shape, q, g, t, 0)] = jnp.where(keep, jnp.where(low, v, vls), 0.0)
            dst_ref[block_at(shape, q, g, t, 1)] = jnp.where(keep, jnp.where(low, vl, vs), 0.0)
            dst_ref[block_at(shape, q, g + 1, t, 0)] = jnp.where(keep, jnp.where(low, vs, vl), 0.0)
            dst_ref[block_at(shape, q, g + 1, t, 1)] = jnp.where(keep, jnp.where(low, vls, v), 0.0)
    each_tile(shape, tile)


def fold(src_ref, dst_ref):
    low = row_iota() < 4
    keep = low == (lane_iota() < 64)
    shape = dst_ref.shape

    def tile(q, t):
        out = []
        for h in range(2):
            e0, o0, e1, o1 = [src_ref[block_at(shape, q, 2 * h + i // 2, t, i % 2)] for i in range(4)]
            stay = jnp.where(keep, jnp.where(low, e0, o1), pltpu.roll(jnp.where(low, o0, e1), 64, 1))
            move = jnp.where(keep, jnp.where(low, e1, o0), pltpu.roll(jnp.where(low, o1, e0), 64, 1))
            out.append(stay + pltpu.roll(move, 4, 0))
        at = pl.ds(pl.multiple_of(t * 128, 128), 128)
        dst_ref[q, :, at] = jnp.concatenate(out, 0).astype(dst_ref.dtype)
    each_tile(shape, tile)


def each_part(blocks, visit):
    def part(i, _):
        visit(pl.ds(i * PART, PART))
        return 0
    lax.fori_loop(0, blocks // PART, part, 0)


def forward_kernel(rows_ref, cols_ref, count_ref, vals_ref, own_ref, packed, fwd_ref, x_col, acc, loose):
    step, steps = pl.program_id(0), pl.num_programs(0)
    nblk = x_col.shape[0]
    quarter = lane_iota() // 32

    @pl.when(step == 0)
    def _():
        expand(own_ref, x_col)

        def clear(at):
            acc[at] = jnp.zeros((PART, 8, 128), F32)
        each_part(nblk, clear)

    count = count_ref[0]
    first = step * CHUNK
    live = jnp.clip(count - first, 0, CHUNK)

    def some_slots(i, _):
        base = i * TOGETHER
        for half in range(TOGETHER // 16):
            z0 = pl.multiple_of(base + half * 16, 16)
            for s in range(32):
                v = vals_ref[pl.ds(z0, 16), s * 128:(s + 1) * 128]
                loose[half, pl.ds(s, 16, stride=32), :] = v.astype(F32)
        for part in range(TOGETHER // 4):
            at = base + part * 4
            w = loose[part // 4, (part % 4) * 128:(part % 4 + 1) * 128, :].astype(BF16)
            packed[pl.ds(pl.multiple_of(at * 32, 128), 128), :] = w
            rows, lf = [], []
            for z in range(4):
                slot = first + at + z
                lf.append(x_col[cols_ref[slot]])
                rows.append(jnp.where(slot < count, rows_ref[slot], nblk))
            of = lax.dot_general(jnp.concatenate(lf, 0).astype(BF16), w, (((1,), (1,)), ((), ())),
                                 preferred_element_type=F32)
            for z in range(4):
                acc[rows[z]] += jnp.where(quarter == z, of[8 * z:8 * z + 8], 0.0)
        return 0
    lax.fori_loop(0, (live + TOGETHER - 1) // TOGETHER, some_slots, 0)

    @pl.when(step == steps - 1)
    def _():
        spread = spread_matrix()

        def part(at):
            x = acc[at].reshape(PART * 8, 128)
            hi = x.astype(BF16)
            lo = (x - hi.astype(F32)).astype(BF16)
            back = (((1,), (1,)), ((), ()))
            y = lax.dot_general(hi, spread, back, preferred_element_type=F32)
            y += lax.dot_general(lo, spread, back, preferred_element_type=F32)
            acc[at] = y.reshape(PART, 8, 128)
        each_part(nblk, part)
        fold(acc, fwd_ref)


def transposed_kernel(rows_ref, cols_ref, count_ref, packed, far_ref, tr_ref, x_row, acc):
    step, steps = pl.program_id(0), pl.num_programs(0)
    nblk = x_row.shape[0]
    quarter = lane_iota() // 32

    @pl.when(step == 0)
    def _():
        expand(far_ref, x_row)
        spread = spread_matrix()

        def part(at):
            x = x_row[at].reshape(PART * 8, 128).astype(BF16)
            x_row[at] = jnp.dot(x, spread, preferred_element_type=F32).reshape(PART, 8, 128)
            acc[at] = jnp.zeros((PART, 8, 128), F32)
        each_part(nblk, part)

    count = count_ref[0]
    first = step * CHUNK
    live = jnp.clip(count - first, 0, CHUNK)

    def some_slots(i, _):
        for part in range(TOGETHER // 4):
            at = i * TOGETHER + part * 4
            w = packed[pl.ds(pl.multiple_of(at * 32, 128), 128), :]
            cols, lt = [], []
            for z in range(4):
                slot = first + at + z
                lt.append(jnp.where(quarter == z, x_row[rows_ref[slot]], 0.0))
                cols.append(jnp.where(slot < count, cols_ref[slot], nblk))
            ot = jnp.dot(jnp.concatenate(lt, 0).astype(BF16), w, preferred_element_type=F32)
            for z in range(4):
                acc[cols[z]] += ot[8 * z:8 * z + 8]
        return 0
    lax.fori_loop(0, (live + TOGETHER - 1) // TOGETHER, some_slots, 0)

    pl.when(step == steps - 1)(lambda: fold(acc, tr_ref))


def cost(slots):
    return pl.CostEstimate(flops=slots * 4 * 128 * 128 * 64, bytes_accessed=slots * 16384, transcendentals=0)


def forward_products(vals, rows, cols, count, own):
    slots, size = vals.shape
    n, depth, width = own.shape
    nblk = n * GROUPS * (width // 64)
    whole = pl.BlockSpec((n, depth, width), lambda i, *_: (0, 0, 0))
    tall = CHUNK * size // 128
    return pl.pallas_call(
        forward_kernel,
        out_shape=(jax.ShapeDtypeStruct((slots * size // 128, 128), BF16), jax.ShapeDtypeStruct(own.shape, BF16)),
        grid_spec=pltpu.PrefetchScalarGridSpec(
            num_scalar_prefetch=3,
            grid=(slots // CHUNK,),
            in_specs=[pl.BlockSpec((CHUNK, size), lambda i, *_: (i, 0)), whole],
            out_specs=(pl.BlockSpec((tall, 128), lambda i, *_: (i, 0)), whole),
            scratch_shapes=[
                pltpu.VMEM((nblk, 8, 128), F32),
                pltpu.VMEM((nblk + 1, 8, 128), F32),
                pltpu.VMEM((TOGETHER // 16, 512, 128), F32),
            ],
        ),
        cost_estimate=cost(slots),
        compiler_params=pltpu.CompilerParams(vmem_limit_bytes=VMEM_BYTES),
    )(rows, cols, count, vals, own)


def transposed_products(packed, rows, cols, count, far):
    slots = rows.shape[0]
    n, depth, width = far.shape
    nblk = n * GROUPS * (width // 64)
    whole = pl.BlockSpec((n, depth, width), lambda i, *_: (0, 0, 0))
    tall = CHUNK * packed.shape[0] // slots
    return pl.pallas_call(
        transposed_kernel,
        out_shape=jax.ShapeDtypeStruct(far.shape, F32),
        grid_spec=pltpu.PrefetchScalarGridSpec(
            num_scalar_prefetch=3,
            grid=(slots // CHUNK,),
            in_specs=[pl.BlockSpec((tall, 128), lambda i, *_: (i, 0)), whole],
            out_specs=whole,
            scratch_shapes=[
                pltpu.VMEM((nblk, 8, 128), F32),
                pltpu.VMEM((nblk + 1, 8, 128), F32),
            ],
        ),
        cost_estimate=cost(slots),
        compiler_params=pltpu.CompilerParams(vmem_limit_bytes=VMEM_BYTES),
    )(rows, cols, count, packed, far)


def reduce_kernel(came_ref, tr_ref, x_ref, res_ref, p_ref, hx_ref, hp_ref, out_ref, sum_ref,
                  stage, landed, part, half, col_slots, row_slots,
                  send, recv, col_send, col_recv, row_send, row_recv):
    n, _, width = came_ref.shape
    vecs, length = x_ref.shape
    cols = lax.axis_size("col")
    r, c = lax.axis_index("row"), lax.axis_index("col")
    barrier = pltpu.get_barrier_semaphore()
    for d in range(1, n):
        pl.semaphore_signal(barrier, inc=1, device_id=(lax.rem(r + d, n), c), device_id_type=MESH)
    for d in range(1, cols):
        pl.semaphore_signal(barrier, inc=1, device_id=(r, lax.rem(c + d, cols)), device_id_type=MESH)

    def row_copy(d):
        return pltpu.make_async_remote_copy(
            src_ref=stage.at[d - 1], dst_ref=landed.at[d - 1],
            send_sem=send.at[d - 1], recv_sem=recv.at[d - 1],
            device_id=(lax.rem(r + d, n), c), device_id_type=MESH)

    def col_sum_copy(d):
        return pltpu.make_async_remote_copy(
            src_ref=part, dst_ref=col_slots.at[c],
            send_sem=col_send.at[d], recv_sem=col_recv.at[d],
            device_id=(r, lax.rem(c + d, cols)), device_id_type=MESH)

    def row_sum_copy(d):
        return pltpu.make_async_remote_copy(
            src_ref=half, dst_ref=row_slots.at[r],
            send_sem=row_send.at[d], recv_sem=row_recv.at[d],
            device_id=(lax.rem(r + d, n), c), device_id_type=MESH)

    def summed(d):
        q = lax.rem(r + d, n)
        return tr_ref[q] + came_ref[q].astype(F32)

    for d in range(1, n):
        stage[d - 1] = summed(d).astype(BF16)
        if d == 1:
            pl.semaphore_wait(barrier, n + cols - 2)
        row_copy(d).start()
    span = min(length, 2048)
    left = [x_ref, res_ref, p_ref]
    right = left + [hx_ref, hp_ref]

    def early(i, gram):
        at = pl.ds(pl.multiple_of(i * span, span), span)
        v = jnp.concatenate([ref[:, at] for ref in left], 0)
        w = jnp.concatenate([ref[:, at] for ref in right], 0)
        return gram + lax.dot_general(v, w, (((1,), (1,)), ((), ())), precision=lax.Precision.HIGHEST,
                                      preferred_element_type=F32)

    part[...] = jnp.zeros_like(part)
    part[:3 * vecs, :5 * vecs] = lax.fori_loop(0, length // span, early, jnp.zeros((3 * vecs, 5 * vecs), F32))
    total = summed(0)
    for d in range(1, n):
        row_copy(d).wait_recv()
        total += landed[d - 1].astype(F32)
    for g in range(GROUPS):
        out_ref[:, g * width:(g + 1) * width] = total[4 * g:4 * g + 4]

    def dots(i, sums):
        sums = list(sums)
        for t in range(8):
            at = pl.ds(pl.multiple_of((i * 8 + t) * 128, 128), 128)
            hw = out_ref[:, at]
            for v in range(3 * vecs):
                row = (x_ref, res_ref, p_ref)[v // vecs][v % vecs:v % vecs + 1, at]
                sums[v] = sums[v] + row * hw
        return tuple(sums)

    sums = lax.fori_loop(0, length // 1024, dots, tuple(jnp.zeros((vecs, 128), F32) for _ in range(3 * vecs)))
    for v in range(3 * vecs):
        part[16:16 + vecs, v:v + 1] = jnp.sum(sums[v], axis=1, keepdims=True)
    for d in range(1, cols):
        col_sum_copy(d).start()
    col_slots[c] = part[...]
    for d in range(1, cols):
        col_sum_copy(d).wait_recv()
    half[...] = jnp.sum(col_slots[...], axis=0)
    for d in range(1, n):
        row_sum_copy(d).start()
    row_slots[r] = half[...]
    for d in range(1, n):
        row_sum_copy(d).wait_recv()
    sum_ref[...] = jnp.sum(row_slots[...], axis=0) * (1.0 / (length * n * cols))

    for d in range(1, n):
        row_copy(d).wait_send()
        row_sum_copy(d).wait_send()
    for d in range(1, cols):
        col_sum_copy(d).wait_send()


def reduce_pieces(came, tr, x_vec, residue, p_vec, hx_vec, hp_vec, cols):
    n, depth, width = came.shape
    vmem = pl.BlockSpec(memory_space=pltpu.VMEM)
    dma = pltpu.SemaphoreType.DMA
    return pl.pallas_call(
        reduce_kernel,
        out_shape=(jax.ShapeDtypeStruct(x_vec.shape, F32), jax.ShapeDtypeStruct(SMALL, F32)),
        in_specs=[vmem] * 7,
        out_specs=(vmem,) * 2,
        scratch_shapes=[
            pltpu.VMEM((n - 1, depth, width), BF16),
            pltpu.VMEM((n - 1, depth, width), BF16),
            pltpu.VMEM(SMALL, F32),
            pltpu.VMEM(SMALL, F32),
            pltpu.VMEM((cols,) + SMALL, F32),
            pltpu.VMEM((n,) + SMALL, F32),
            dma((n - 1,)), dma((n - 1,)),
            dma((cols,)), dma((cols,)), dma((n,)), dma((n,)),
        ],
        compiler_params=pltpu.CompilerParams(
            collective_id=1, has_side_effects=True, vmem_limit_bytes=VMEM_BYTES),
    )(came, tr, x_vec, residue, p_vec, hx_vec, hp_vec)


def finish_kernel(hw_ref, sum_ref, out_ref, a_ref, b_ref):
    out_ref[...] = hw_ref[...]
    vecs = hw_ref.shape[0]
    basis = 3 * vecs
    gram = sum_ref[...]
    b_ref[...] = gram[:basis, :basis]
    a_ref[:, :vecs] = gram[:basis, basis:basis + vecs]
    turned = jnp.transpose(gram[16:24])
    a_ref[:, vecs:2 * vecs] = turned[:basis, :vecs]
    a_ref[:, 2 * vecs:] = gram[:basis, basis + vecs:basis + 2 * vecs]


def finish(hw_vec, gram):
    basis = 3 * hw_vec.shape[0]
    vmem = pl.BlockSpec(memory_space=pltpu.VMEM)
    square = jax.ShapeDtypeStruct((basis, basis), F32)
    return pl.pallas_call(
        finish_kernel,
        out_shape=(jax.ShapeDtypeStruct(hw_vec.shape, F32), square, square),
        in_specs=[vmem] * 2,
        out_specs=(vmem,) * 3,
    )(hw_vec, gram)


def body(x_vec, hx_vec, p_vec, hp_vec, theta, precond, tile_vals, tile_rows, tile_cols, tile_count):
    n = lax.axis_size("row")
    cols = lax.axis_size("col")
    places = [(r, c) for r in range(n) for c in range(cols)]
    down = [(r * cols + (c + r) % cols, r * cols + c) for r, c in places]
    up = [(target, source) for source, target in down]
    rows, columns, count = tile_rows[0, 0], tile_cols[0, 0], tile_count[0]
    own, residue = gather_pieces(x_vec, hx_vec, theta, precond, n)
    far = lax.ppermute(own, ("row", "col"), down)
    packed, fwd = forward_products(tile_vals[0, 0], rows, columns, count, own)
    came = lax.ppermute(fwd, ("row", "col"), up)
    tr = transposed_products(packed, rows, columns, count, far)
    hw_vec, gram = reduce_pieces(came, tr, x_vec, residue, p_vec, hx_vec, hp_vec, cols)
    return finish(hw_vec, gram)


def solution(mesh):
    placed = (
        P(None, ("col", "row")),
        P(None, ("col", "row")),
        P(None, ("col", "row")),
        P(None, ("col", "row")),
        P(),
        P(("col", "row")),
        P("row", "col", None, None),
        P("row", "col", None),
        P("row", "col", None),
        P("row", "col"),
    )
    return jax.shard_map(
        body,
        mesh=mesh,
        in_specs=placed,
        out_specs=(P(None, ("col", "row")), P(), P()),
        check_vma=False,
    )
```
